32 devices in a mesh: slab: 8 (over y, x, core), grp: 4 (over z).
Axes of the slice: x: 2, y: 2, z: 4, core: 2. Of those that a mesh axis runs over, the one named last changes fastest.
Arguments:
- cloud_states: float32 [2, 16, 4, 64, 1024], P(None, 'grp', None, 'slab'), may hold values from -6 to 6
- cloud_shift: int32 [2], replicated, may hold values from 9 to 15, as said below
- boost_wave: int32 [2], replicated, may hold values from -6 to 6, as said below
Outputs:
- evolved: float32 [2, 16, 4, 64, 1024], P(None, 'grp', None, 'slab')
The draws below stay inside these ranges and needn't reach their ends.
Inputs may be any that keep to these rules, and one draw needn't show every extreme that they name: `cloud_shift`: one of the two entries equals 15. `boost_wave`: the first entry is 6; the second is negative.
All inputs are finite; a program needn't handle non-finite values.
Results may differ from the reference program's by a relative error of at most 0.00002.
Values sent between devices are 32-bit elements; how exact they have to be, the bound alone decides.
No kernel may reach another device: no remote copies, remote signals or barrier semaphores. Data moves between devices by JAX's collectives and lax.ppermute only.
A program may use at most 64 MiB of HBM per device.

```python
import math
import jax
import jax.numpy as jnp
from jax import lax

NY = 32
CZ = 8
NXY = 1024
NZ = 64
S = 16


def draw_cloud_shift(key, part):
    key_other = jax.random.fold_in(key, 11)
    key_which = jax.random.fold_in(key, 12)
    other_shift = jax.random.randint(key_other, (), CZ + 1, 2 * CZ, dtype=jnp.int32)
    which_first = jax.random.randint(key_which, (), 0, 2, dtype=jnp.int32)
    largest_shift = jnp.full((), 2 * CZ - 1, dtype=jnp.int32)
    return jnp.where(which_first == 0, jnp.stack([largest_shift, other_shift]), jnp.stack([other_shift, largest_shift])).astype(jnp.int32)


def draw_boost_wave(key, part):
    key_second = jax.random.fold_in(key, 21)
    second_wave = -jax.random.randint(key_second, (), 1, 7, dtype=jnp.int32)
    first_wave = jnp.full((), 6, dtype=jnp.int32)
    return jnp.stack([first_wave, second_wave]).astype(jnp.int32)


def levels(own_key, dims, shards, least, high):
    loudness, own = 1.0, jax.random.fold_in(own_key, 6)
    for dim, shards_of in shards:
        steps = jnp.exp(jax.random.uniform(jax.random.fold_in(own, dim), (shards_of,), jnp.float32, least / len(shards), high / len(shards)))
        loudness = loudness * jnp.repeat(steps, dims[dim] // shards_of).reshape([-1 if axis == dim else 1 for axis in range(len(dims))])
    return loudness


def scatter_about(key, extent, scale, bound, pieces=(), held_as=jnp.bfloat16):
    array = jax.random.normal(key, extent, jnp.float32) * scale
    if len(pieces) > 0:
        array = levels(key, extent, pieces, -0.22, 0.18) * array
    return jnp.clip(array, min=-bound, max=bound).astype(held_as)


def setup_inputs(seed: int = 0) -> dict:
    streams_of = jax.random.split(jax.random.key(seed), 4)
    cloud_states = scatter_about(streams_of[0], (2, S, 4, NZ, NXY), 1.0, 6.0, ((1, 4), (3, 8)), jnp.float32)
    cloud_shift = draw_cloud_shift(jax.random.fold_in(streams_of[3], 71), 0)
    boost_wave = draw_boost_wave(jax.random.fold_in(streams_of[3], 71), 0)
    return {"cloud_states": cloud_states, "cloud_shift": cloud_shift, "boost_wave": boost_wave}


stencil = (-49.0 / 18.0, 1.5, -0.15, 1.0 / 90.0)
coupling = 3.0
xi_factor = 1.2
chemical = 1.0
time_step = 0.1


def transverse(volume, row_width):
    cell_count = volume.shape[-1]
    column = lax.broadcasted_iota(jnp.int32, (cell_count,), 0) % row_width
    pad_spec = [(0, 0)] * (volume.ndim - 1) + [(3 * row_width, 3 * row_width)]
    padded = jnp.pad(volume, pad_spec)
    running = 2.0 * stencil[0] * volume
    base = 3 * row_width
    for offset in range(1, 4):
        for signed in (offset, -offset):
            across_rows = padded[..., base + signed * row_width: base + signed * row_width + cell_count]
            across_columns = padded[..., base + signed: base + signed + cell_count]
            inside = ((column + signed >= 0) & (column + signed < row_width)).astype(jnp.float32)
            running = running + stencil[offset] * (across_rows + across_columns * inside)
    return running


def along_depth(extended, planes):
    running = stencil[0] * extended[..., 3:3 + planes, :]
    for offset in range(1, 4):
        for signed in (offset, -offset):
            running = running + stencil[offset] * extended[..., 3 + signed:3 + signed + planes, :]
    return running


def laplacian(single):
    padded = jnp.pad(single, ((0, 0), (3, 3), (0, 0)), mode="wrap")
    return along_depth(padded, single.shape[1]) + transverse(single, NY)


def fields_of(totals):
    potential = xi_factor * jnp.square(jnp.cbrt(totals[0])) - chemical
    return jnp.stack([potential, -coupling * totals[1], -coupling * totals[2]])


def potentials(states):
    particle_real = states[:, 0]
    particle_imag = states[:, 1]
    hole_real = states[:, 2]
    hole_imag = states[:, 3]
    density = jnp.sum(hole_real * hole_real + hole_imag * hole_imag, axis=0) / S
    pair_real = jnp.sum(particle_real * hole_real + particle_imag * hole_imag, axis=0) / S
    pair_imag = jnp.sum(particle_imag * hole_real - particle_real * hole_imag, axis=0) / S
    return fields_of(jnp.stack([density, pair_real, pair_imag]))


def hamiltonian(single, fields):
    kinetic = -0.5 * laplacian(single)
    potential = fields[0]
    gap_real = fields[1]
    gap_imag = fields[2]
    particle_real, particle_imag, hole_real, hole_imag = single[0], single[1], single[2], single[3]
    out_pr = kinetic[0] + potential * particle_real + gap_real * hole_real - gap_imag * hole_imag
    out_pi = kinetic[1] + potential * particle_imag + gap_real * hole_imag + gap_imag * hole_real
    out_hr = gap_real * particle_real + gap_imag * particle_imag - kinetic[2] - potential * hole_real
    out_hi = gap_real * particle_imag - gap_imag * particle_real - kinetic[3] - potential * hole_imag
    return jnp.stack([out_pr, out_pi, out_hr, out_hi])


def advance(single, change, factor):
    return jnp.stack([single[0] + factor * change[1], single[1] - factor * change[0],
                      single[2] + factor * change[3], single[3] - factor * change[2]])


def reference(cloud_states, cloud_shift, boost_wave):
    planes = jnp.arange(NZ, dtype=jnp.int32)
    source_first = jnp.mod(planes - cloud_shift[0], NZ).astype(jnp.int32)
    source_second = jnp.mod(planes + cloud_shift[1], NZ).astype(jnp.int32)
    first_cloud = jnp.take(cloud_states[0], source_first, axis=2)
    second_cloud = jnp.take(cloud_states[1], source_second, axis=2)
    placed = jnp.stack([first_cloud, second_cloud])
    phase_index = jnp.mod(boost_wave[:, None] * planes[None, :], NZ)
    phases = (2.0 * math.pi / NZ) * phase_index.astype(jnp.float32)
    cosine_table = jnp.cos(phases)[:, None, :, None]
    sine_table = jnp.sin(phases)[:, None, :, None]
    particle_real = placed[:, :, 0]
    particle_imag = placed[:, :, 1]
    hole_real = placed[:, :, 2]
    hole_imag = placed[:, :, 3]
    boosted = jnp.stack([particle_real * cosine_table - particle_imag * sine_table,
                         particle_real * sine_table + particle_imag * cosine_table,
                         hole_real * cosine_table + hole_imag * sine_table,
                         hole_imag * cosine_table - hole_real * sine_table], axis=2)
    flat_states = boosted.reshape(2 * S, 4, NZ, NXY)
    fields_now = potentials(flat_states)

    def predict_one(single):
        return advance(single, hamiltonian(single, fields_now), time_step)

    predicted = lax.map(predict_one, flat_states)
    fields_next = potentials(predicted)

    def correct_one(couple):
        change = hamiltonian(couple[0], fields_now) + hamiltonian(couple[1], fields_next)
        return advance(couple[0], change, time_step / 2.0)

    evolved = lax.map(correct_one, (flat_states, predicted))
    return evolved.reshape(2, S, 4, NZ, NXY)
```

```python
import functools
import math

import jax
import jax.numpy as jnp
import numpy as np
from jax import lax
from jax.experimental import pallas as pl
from jax.experimental.pallas import tpu as pltpu
from jax.sharding import PartitionSpec as P

NY = 32
LANES = 128
SUBS = 8
HALO = 3
REACH = 2 * HALO
CHUNKS = 2
VMEM_BYTES = 40 * 1024 * 1024

stencil = (-49.0 / 18.0, 1.5, -0.15, 1.0 / 90.0)
coupling = 3.0
xi_factor = 1.2
chemical = 1.0
time_step = 0.1

VMEM = pl.BlockSpec(memory_space=pltpu.VMEM)
SMEM = pl.BlockSpec(memory_space=pltpu.SMEM)


def params():
    return pltpu.CompilerParams(vmem_limit_bytes=VMEM_BYTES)


def moved(x, axis, by):
    peers = lax.axis_size(axis)
    return lax.ppermute(x, axis, [(i, (i + by) % peers) for i in range(peers)])


def swapped(x):
    peers = lax.axis_size("slab")
    return lax.ppermute(x, "slab", [(i, i ^ 1) for i in range(peers)])


def transverse_weights():
    whole = {0: -980.0, 1: 270.0, 2: -27.0, 3: 2.0}
    rows = LANES // NY
    weights = np.zeros((LANES, 3 * LANES), np.float32)
    for a in range(LANES):
        xa, ya = divmod(a, NY)
        for b in range(LANES):
            xb, yb = divmod(b, NY)
            for part, distance in ((0, xb + rows - xa), (1, xb - xa), (2, xb - rows - xa)):
                if ya == yb and abs(distance) <= HALO:
                    weights[a, part * LANES + b] += whole[abs(distance)]
            if xa == xb and 0 < abs(ya - yb) <= HALO:
                weights[a, LANES + b] += whole[abs(ya - yb)]
    return np.concatenate([weights, weights]).astype(jnp.bfloat16)


def phase(wave, first, depth):
    z = first + lax.broadcasted_iota(jnp.int32, (SUBS, LANES), 0)
    index = jnp.bitwise_and(wave * z, depth - 1)
    angle = (2.0 * math.pi / depth) * index.astype(jnp.float32)
    return jnp.cos(angle), jnp.sin(angle)


def densities(ur, ui, vr, vi):
    return vr * vr + vi * vi, ur * vr + ui * vi, ui * vr - ur * vi


def fields_of(n, kr, ki, scale):
    n = n * scale
    safe = jnp.where(n > 0.0, n, 1.0)
    power = jnp.where(n > 0.0, jnp.exp((2.0 / 3.0) * jnp.log(safe)), 0.0)
    return xi_factor * power - chemical, (-coupling * scale) * kr, (-coupling * scale) * ki


def local_part(field, ur, ui, vr, vi):
    potential, gap_real, gap_imag = field
    return (
        potential * ur + gap_real * vr - gap_imag * vi,
        potential * ui + gap_real * vi + gap_imag * vr,
        gap_real * ur + gap_imag * ui - potential * vr,
        gap_real * ui - gap_imag * ur - potential * vi,
    )


def raw_density_kernel(parts, me_ref, x_ref, *refs):
    outs, total = refs[:-1], refs[-1]
    clouds, states, _, planes, cells = x_ref.shape
    for j in range(clouds):
        for t in range(cells // LANES):
            lanes = pl.ds(t * LANES, LANES)
            sums = [jnp.zeros((planes, LANES), jnp.float32)] * 3
            for s in range(states):
                terms = densities(*[x_ref[j, s, k, :, lanes] for k in range(4)])
                sums = [a + b for a, b in zip(sums, terms)]
            for f in range(3):
                total[j, f, :, lanes] = sums[f]
    width = cells // parts
    for d in range(parts):
        first = pl.multiple_of(lax.rem(me_ref[0] + d, parts) * width, width)
        outs[d][...] = total[:, :, :, pl.ds(first, width)]


def raw_density(x, me, parts):
    clouds, _, _, planes, cells = x.shape
    shape = jax.ShapeDtypeStruct((clouds, 3, planes, cells // parts), jnp.float32)
    return pl.pallas_call(
        functools.partial(raw_density_kernel, parts),
        out_shape=[shape] * parts,
        in_specs=[SMEM, VMEM],
        out_specs=[VMEM] * parts,
        scratch_shapes=[pltpu.VMEM((clouds, 3, planes, cells), jnp.float32)],
        compiler_params=params(),
        name="raw_density",
    )(me, x)


def placed_fields_kernel(depth, scale, where_ref, shift_ref, wave_ref, *refs):
    first_refs, second_refs = refs[0:4], refs[4:8]
    out_ref, held = refs[8], refs[9]
    planes = first_refs[0].shape[1]
    width = first_refs[0].shape[2]
    slab = where_ref[0]
    for j, slots in enumerate((first_refs, second_refs)):
        for q, slot in enumerate(slots):
            first = (slab - 3 + q) * planes + shift_ref[0] if j == 0 else (slab + q) * planes - shift_ref[1]
            cos, sin = phase(2 * wave_ref[j], first, depth)
            for t in range(width // LANES):
                lanes = pl.ds(t * LANES, LANES)
                kr, ki = slot[1, :, lanes], slot[2, :, lanes]
                layers = pl.ds(q * planes, planes)
                held[j, 0, layers, lanes] = slot[0, :, lanes]
                held[j, 1, layers, lanes] = kr * cos - ki * sin
                held[j, 2, layers, lanes] = kr * sin + ki * cos
    count = out_ref.shape[1]
    start_first = 3 * planes - HALO - shift_ref[0]
    start_second = shift_ref[1] - HALO
    rows = held.shape[2]
    totals = [
        pltpu.roll(held[0, f], rows - start_first, 0)[:count] + pltpu.roll(held[1, f], rows - start_second, 0)[:count] for f in range(3)
    ]
    for f, field in enumerate(fields_of(*totals, scale)):
        out_ref[f] = field


def placed_fields(where, shift, wave, first, second, depth, scale):
    planes, width = first[0].shape[1:]
    return pl.pallas_call(
        functools.partial(placed_fields_kernel, depth, scale),
        out_shape=jax.ShapeDtypeStruct((3, planes + 8, width), jnp.float32),
        in_specs=[SMEM] * 3 + [VMEM] * 8,
        out_specs=VMEM,
        scratch_shapes=[pltpu.VMEM((2, 3, 4 * planes, width), jnp.float32)],
        compiler_params=params(),
        name="placed_fields",
    )(where, shift, wave, *first, *second)


def transverse(x, weights):
    rows = x.shape[0]
    flat = x.reshape(rows * SUBS, LANES)
    high = flat.astype(jnp.bfloat16)
    low = (flat - high.astype(jnp.float32)).astype(jnp.bfloat16)
    product = jnp.dot(jnp.concatenate([high, low], axis=1), weights, preferred_element_type=jnp.float32)
    sub = lax.broadcasted_iota(jnp.int32, (rows * SUBS, LANES), 0) % SUBS
    up = pltpu.roll(product[:, :LANES].reshape(rows, SUBS, LANES), 1, 1).reshape(rows * SUBS, LANES)
    down = pltpu.roll(product[:, 2 * LANES :].reshape(rows, SUBS, LANES), SUBS - 1, 1).reshape(rows * SUBS, LANES)
    result = product[:, LANES : 2 * LANES] + jnp.where(sub > 0, up, 0.0) + jnp.where(sub < SUBS - 1, down, 0.0)
    return result.reshape(rows, SUBS, LANES)


def kinetic(layers, weights):
    count = layers.shape[0] - 2 * HALO
    inner = layers[HALO : HALO + count]
    along = stencil[0] * inner
    for j in range(1, HALO + 1):
        along = along + stencil[j] * (layers[HALO - j : HALO - j + count] + layers[HALO + j : HALO + j + count])
    return -0.5 * along + (-0.5 / 180.0) * transverse(inner, weights)


def gather_kernel(depth, where_ref, shift_ref, wave_ref, weights_ref, own_ref, partner_ref, extra_ref, recv_first, recv_second,
                  precv_first, precv_second, boosted_ref, base_ref, window):
    slab = where_ref[0]
    even = lax.rem(slab, 2) == 0
    planes = own_ref.shape[3]
    states = own_ref.shape[1]
    tiles = own_ref.shape[4] // LANES
    count = boosted_ref.shape[3]

    def turned(u_re, u_im, v_re, v_im, cos, sin):
        return u_re * cos - u_im * sin, u_re * sin + u_im * cos, v_re * cos + v_im * sin, v_im * cos - v_re * sin

    for j in range(2):
        phases = []
        for q in range(4):
            first = (slab - 3 + q) * planes + shift_ref[0] if j == 0 else (slab + q) * planes - shift_ref[1]
            phases.append(phase(wave_ref[j], first, depth))
        start = 3 * planes - REACH - shift_ref[0] if j == 0 else shift_ref[1] - REACH

        def one_state(s, _):
            def fill(q, read):
                cos, sin = phases[q]
                for t in range(tiles):
                    lanes = pl.ds(t * LANES, LANES)
                    for k, value in enumerate(turned(*[read(k, lanes) for k in range(4)], cos, sin)):
                        window[k, pl.ds(q * planes, planes), t, :] = value

            def fill_extra(q, layer):
                cos, sin = phases[q]
                for n in range(extra_ref.shape[2]):
                    inside = layer % planes + n
                    c = jnp.broadcast_to(cos[inside : inside + 1], (SUBS, LANES))
                    d = jnp.broadcast_to(sin[inside : inside + 1], (SUBS, LANES))
                    for k, value in enumerate(turned(*[extra_ref[s, k, n] for k in range(4)], c, d)):
                        window[k, layer + n] = value

            own = lambda k, lanes: own_ref[j, s, k, :, lanes]
            partner = lambda k, lanes: partner_ref[j, s, k, :, lanes]
            recv = lambda k, lanes: (recv_first if j == 0 else recv_second)[s, k, :, lanes]
            precv = lambda k, lanes: (precv_first if j == 0 else precv_second)[s, k, :, lanes]
            far = 0 if j == 0 else 3
            near = 2 if j == 0 else 1
            fill(3 - far, own)
            fill(3 - near, recv)

            @pl.when(even if j == 0 else jnp.logical_not(even))
            def _():
                fill(near, precv)
                fill_extra(far, planes - extra_ref.shape[2] if j == 0 else 3 * planes)

            @pl.when(jnp.logical_not(even) if j == 0 else even)
            def _():
                fill(near, partner)
                fill(far, precv)

            kin = []
            values = []
            for k in range(4):
                layers = window[k, pl.ds(start, count + 2 * HALO)]
                values.append(layers[HALO : HALO + count])
                kin.append(kinetic(layers, weights_ref[...]))
            for k in range(4):
                boosted_ref[j, s, k] = values[k]
            base_ref[j, s, 0] = values[0] + time_step * kin[1]
            base_ref[j, s, 1] = values[1] - time_step * kin[0]
            base_ref[j, s, 2] = values[2] - time_step * kin[3]
            base_ref[j, s, 3] = values[3] + time_step * kin[2]
            return 0

        lax.fori_loop(0, states, one_state, 0)


def gather(where, shift, wave, weights, x, partner, extra, received, exchanged, chunk, depth):
    _, per_group, _, planes, cells = x.shape
    states = per_group // CHUNKS
    count = planes + 2 * HALO
    shape = jax.ShapeDtypeStruct((2, states, 4, count, SUBS, LANES), jnp.float32)
    five = lambda block: pl.BlockSpec(block, lambda i: (0, chunk, 0, 0, 0))
    whole = lambda a: pl.BlockSpec(a.shape, lambda i: (0,) * a.ndim)
    extra_spec = pl.BlockSpec((states, *extra.shape[1:]), lambda i: (chunk, 0, 0, 0, 0))
    operands = (*received, *exchanged)
    return pl.pallas_call(
        functools.partial(gather_kernel, depth),
        out_shape=[shape] * 2,
        grid=(1,),
        in_specs=[SMEM] * 3 + [whole(weights), five((2, states, 4, planes, cells)), five((2, states, 4, planes, cells)), extra_spec]
        + [whole(a) for a in operands],
        out_specs=[pl.BlockSpec(shape.shape, lambda i: (0,) * 6)] * 2,
        scratch_shapes=[pltpu.VMEM((4, 4 * planes, SUBS, LANES), jnp.float32)],
        compiler_params=params(),
        name="gather",
    )(where, shift, wave, weights, x, partner, extra, *operands)


def spread_fields(me_ref, parts, field_refs, fields):
    count = fields.shape[1]
    width = field_refs[0].shape[2]
    tiles = width // LANES
    for d, ref in enumerate(field_refs):
        part = lax.rem(me_ref[0] + parts - d, parts)
        for own in range(parts):
            @pl.when(part == own)
            def _():
                for f in range(3):
                    for t in range(tiles):
                        fields[f, :, own * tiles + t, :] = ref[f, 0:count, t * LANES : (t + 1) * LANES]


def density_kernel(parts, chunks, me_ref, *refs):
    field_refs = refs[:parts]
    boosted_refs = refs[parts : parts + chunks]
    base_refs = refs[parts + chunks : parts + 2 * chunks]
    out_ref, fields, sums = refs[parts + 2 * chunks :]
    spread_fields(me_ref, parts, field_refs, fields)
    planes = sums.shape[1]
    states = boosted_refs[0].shape[1]
    for z in range(planes):
        field = [fields[f, HALO + z] for f in range(3)]
        total = [jnp.zeros((SUBS, LANES), jnp.float32)] * 3
        for boosted, base in zip(boosted_refs, base_refs):
            for j in range(2):
                for s in range(states):
                    part = local_part(field, *[boosted[j, s, k, HALO + z] for k in range(4)])
                    pr = base[j, s, 0, HALO + z] + time_step * part[1]
                    pi = base[j, s, 1, HALO + z] - time_step * part[0]
                    hr = base[j, s, 2, HALO + z] + time_step * part[3]
                    hi = base[j, s, 3, HALO + z] - time_step * part[2]
                    total = [a + b for a, b in zip(total, densities(pr, pi, hr, hi))]
        for f in range(3):
            sums[f, z] = total[f]
    for f in range(3):
        for t in range(SUBS):
            out_ref[f, :, t * LANES : (t + 1) * LANES] = sums[f, :, t, :]


def density(me, fields, boosted, base, planes):
    parts, chunks = len(fields), len(boosted)
    return pl.pallas_call(
        functools.partial(density_kernel, parts, chunks),
        out_shape=jax.ShapeDtypeStruct((3, planes, SUBS * LANES), jnp.float32),
        in_specs=[SMEM] + [VMEM] * (parts + 2 * chunks),
        out_specs=VMEM,
        scratch_shapes=[
            pltpu.VMEM((3, planes + 2 * HALO, SUBS, LANES), jnp.float32),
            pltpu.VMEM((3, planes, SUBS, LANES), jnp.float32),
        ],
        compiler_params=params(),
        name="density",
    )(me, *fields, *boosted, *base)


def free_kernel(parts, chunks, me_ref, weights_ref, *refs):
    field_refs = refs[:parts]
    boosted_refs = refs[parts : parts + chunks]
    base_refs = refs[parts + chunks : parts + 2 * chunks]
    free_ref, predicted_ref, fields, window, turned = refs[parts + 2 * chunks :]
    spread_fields(me_ref, parts, field_refs, fields)
    planes = free_ref.shape[3]
    states = boosted_refs[0].shape[1]
    inner = pl.ds(HALO, planes)
    for c, (boosted, base) in enumerate(zip(boosted_refs, base_refs)):
        for j in range(2):
            def one_state(s, _):
                for z in range(planes + 2 * HALO):
                    field = [fields[f, z] for f in range(3)]
                    part = local_part(field, *[boosted[j, s, k, z] for k in range(4)])
                    window[0, z] = base[j, s, 0, z] + time_step * part[1]
                    window[1, z] = base[j, s, 1, z] - time_step * part[0]
                    window[2, z] = base[j, s, 2, z] + time_step * part[3]
                    window[3, z] = base[j, s, 3, z] - time_step * part[2]
                kin = [kinetic(window[k], weights_ref[...]) for k in range(4)]
                mean = [0.5 * (boosted[j, s, k, inner] + window[k, inner]) for k in range(4)]
                half = 0.5 * time_step
                turned[0] = mean[0] + half * kin[1]
                turned[1] = mean[1] - half * kin[0]
                turned[2] = mean[2] - half * kin[3]
                turned[3] = mean[3] + half * kin[2]
                for k in range(4):
                    for t in range(SUBS):
                        lanes = pl.ds(t * LANES, LANES)
                        free_ref[j, c * states + s, k, :, lanes] = turned[k, :, t, :]
                        predicted_ref[j, c * states + s, k, :, lanes] = window[k, inner, t, :]
                return 0

            lax.fori_loop(0, states, one_state, 0)


def free_part(me, weights, fields, boosted, base, shape, planes):
    parts, chunks = len(fields), len(boosted)
    out = jax.ShapeDtypeStruct(shape, jnp.float32)
    return pl.pallas_call(
        functools.partial(free_kernel, parts, chunks),
        out_shape=[out] * 2,
        in_specs=[SMEM] + [VMEM] * (1 + parts + 2 * chunks),
        out_specs=[VMEM] * 2,
        scratch_shapes=[
            pltpu.VMEM((3, planes + 2 * HALO, SUBS, LANES), jnp.float32),
            pltpu.VMEM((4, planes + 2 * HALO, SUBS, LANES), jnp.float32),
            pltpu.VMEM((4, planes, SUBS, LANES), jnp.float32),
        ],
        compiler_params=params(),
        name="free_part",
    )(me, weights, *fields, *boosted, *base)


def last_kernel(scale, *refs):
    partial_refs = refs[:-4]
    free_ref, predicted_ref, out_ref, fields = refs[-4:]

    @pl.when(pl.program_id(0) == 0)
    def _():
        totals = []
        for f in range(3):
            total = partial_refs[0][f]
            for ref in partial_refs[1:]:
                total = total + ref[f]
            totals.append(total)
        for f, field in enumerate(fields_of(*totals, scale)):
            fields[f] = field

    half = 0.5 * time_step
    for t in range(free_ref.shape[-1] // LANES):
        lanes = pl.ds(t * LANES, LANES)
        field = [fields[f, :, lanes] for f in range(3)]
        for s in range(free_ref.shape[1]):
            part = local_part(field, *[predicted_ref[0, s, k, :, lanes] for k in range(4)])
            out_ref[0, s, 0, :, lanes] = free_ref[0, s, 0, :, lanes] + half * part[1]
            out_ref[0, s, 1, :, lanes] = free_ref[0, s, 1, :, lanes] - half * part[0]
            out_ref[0, s, 2, :, lanes] = free_ref[0, s, 2, :, lanes] + half * part[3]
            out_ref[0, s, 3, :, lanes] = free_ref[0, s, 3, :, lanes] - half * part[2]


def last_part(partials, free, predicted, scale):
    shape = free.shape
    whole = pl.BlockSpec(partials[0].shape, lambda i: (0, 0, 0))
    block = pl.BlockSpec((1, *shape[1:]), lambda i: (i, 0, 0, 0, 0))
    return pl.pallas_call(
        functools.partial(last_kernel, scale),
        out_shape=jax.ShapeDtypeStruct(shape, jnp.float32),
        grid=(shape[0],),
        in_specs=[whole] * len(partials) + [block] * 2,
        out_specs=block,
        scratch_shapes=[pltpu.VMEM(partials[0].shape, jnp.float32)],
        compiler_params=params(),
        name="last_part",
    )(*partials, free, predicted)


def local(weights, cloud_states, cloud_shift, boost_wave):
    slab_count, group_count = lax.axis_size("slab"), lax.axis_size("grp")
    _, per_group, _, planes, cells = cloud_states.shape
    depth = planes * slab_count
    scale = 1.0 / (per_group * group_count)
    few = group_count <= 4 and cells % (group_count * LANES) == 0
    parts = group_count if few else 1
    slab = lax.axis_index("slab")
    where = slab.astype(jnp.int32).reshape(1)
    me = lax.axis_index("grp").astype(jnp.int32).reshape(1)

    own = raw_density(cloud_states, me, parts)
    if few:
        summed = own[0]
        for d in range(1, parts):
            summed = summed + moved(own[d], "grp", d)
    else:
        summed = lax.psum(own[0], "grp")

    per_chunk = per_group // CHUNKS
    received = []
    for c in range(CHUNKS):
        states = slice(c * per_chunk, (c + 1) * per_chunk)
        received.append((moved(cloud_states[0, states], "slab", 2), moved(cloud_states[1, states], "slab", -2)))
    partner = swapped(cloud_states)
    odd = lax.rem(slab, 2) == 1
    extra_layers = REACH - 1
    leaving = jnp.where(odd, cloud_states[0, :, :, planes - extra_layers :], cloud_states[1, :, :, :extra_layers])
    leaving = leaving.reshape(per_group, 4, extra_layers, SUBS, LANES)
    extra = lax.ppermute(leaving, "slab", [(i, (i + 3) % slab_count if i % 2 else (i - 3) % slab_count) for i in range(slab_count)])

    first = [moved(summed[0], "slab", d) for d in (3, 2, 1)] + [summed[0]]
    second = [summed[1]] + [moved(summed[1], "slab", -d) for d in (1, 2, 3)]
    piece = placed_fields(where, cloud_shift, boost_wave, first, second, depth, scale)
    fields = [piece] + [moved(piece, "grp", d) for d in range(1, parts)]

    boosted, base = [], []
    for c in range(CHUNKS):
        exchanged = [swapped(r) for r in received[c]]
        b, a = gather(where, cloud_shift, boost_wave, weights, cloud_states, partner, extra, received[c], exchanged, c, depth)
        boosted.append(b)
        base.append(a)
    partial = density(me, fields, boosted, base, planes)
    if few:
        partials = [partial] + [moved(partial, "grp", d) for d in range(1, parts)]
    else:
        partials = [lax.psum(partial, "grp")]
    free, predicted = free_part(me, weights, fields, boosted, base, cloud_states.shape, planes)
    return last_part(partials, free, predicted, scale)


def solution(mesh):
    states = P(None, "grp", None, "slab", None)
    weights = transverse_weights()
    step = jax.shard_map(local, mesh=mesh, in_specs=(P(), states, P(), P()), out_specs=states, check_vma=False)
    return lambda cloud_states, cloud_shift, boost_wave: step(weights, cloud_states, cloud_shift, boost_wave)
```

```python
import functools
import math

import jax
import jax.numpy as jnp
import numpy as np
from jax import lax
from jax.experimental import pallas as pl
from jax.experimental.pallas import tpu as pltpu
from jax.sharding import PartitionSpec as P

NY = 32
LANES = 128
SUBS = 8
HALO = 3
REACH = 2 * HALO
VMEM_BYTES = 40 * 1024 * 1024

stencil = (-49.0 / 18.0, 1.5, -0.15, 1.0 / 90.0)
coupling = 3.0
xi_factor = 1.2
chemical = 1.0
time_step = 0.1

VMEM = pl.BlockSpec(memory_space=pltpu.VMEM)
SMEM = pl.BlockSpec(memory_space=pltpu.SMEM)
ANYWHERE = pl.BlockSpec(memory_space=pl.ANY)


def params():
    return pltpu.CompilerParams(vmem_limit_bytes=VMEM_BYTES)


def moved(x, axis, by):
    peers = lax.axis_size(axis)
    return lax.ppermute(x, axis, [(i, (i + by) % peers) for i in range(peers)])


def swapped(x):
    peers = lax.axis_size("slab")
    return lax.ppermute(x, "slab", [(i, i ^ 1) for i in range(peers)])


def transverse_weights():
    whole = {0: -980.0, 1: 270.0, 2: -27.0, 3: 2.0}
    rows = LANES // NY
    weights = np.zeros((LANES, 3 * LANES), np.float32)
    for a in range(LANES):
        xa, ya = divmod(a, NY)
        for b in range(LANES):
            xb, yb = divmod(b, NY)
            for part, distance in ((0, xb + rows - xa), (1, xb - xa), (2, xb - rows - xa)):
                if ya == yb and abs(distance) <= HALO:
                    weights[a, part * LANES + b] += whole[abs(distance)]
            if xa == xb and 0 < abs(ya - yb) <= HALO:
                weights[a, LANES + b] += whole[abs(ya - yb)]
    return np.concatenate([weights, weights]).astype(jnp.bfloat16)


def phase(wave, first, depth):
    z = first + lax.broadcasted_iota(jnp.int32, (SUBS, LANES), 0)
    index = jnp.bitwise_and(wave * z, depth - 1)
    angle = (2.0 * math.pi / depth) * index.astype(jnp.float32)
    return jnp.cos(angle), jnp.sin(angle)


def densities(ur, ui, vr, vi):
    return vr * vr + vi * vi, ur * vr + ui * vi, ui * vr - ur * vi


def fields_of(n, kr, ki, scale):
    n = n * scale
    safe = jnp.where(n > 0.0, n, 1.0)
    power = jnp.where(n > 0.0, jnp.exp((2.0 / 3.0) * jnp.log(safe)), 0.0)
    return xi_factor * power - chemical, (-coupling * scale) * kr, (-coupling * scale) * ki


def local_part(field, ur, ui, vr, vi):
    potential, gap_real, gap_imag = field
    return (
        potential * ur + gap_real * vr - gap_imag * vi,
        potential * ui + gap_real * vi + gap_imag * vr,
        gap_real * ur + gap_imag * ui - potential * vr,
        gap_real * ui - gap_imag * ur - potential * vi,
    )


def copy_rows(x_ref, cloud, state, out_ref, first_row):
    planes, cells = x_ref.shape[3:]
    for k in range(4):
        rows = pl.ds(first_row + k * planes, planes)
        for t in range(cells // LANES):
            out_ref[rows, t, :] = x_ref[cloud, state, k, :, t * LANES : (t + 1) * LANES]


def take_kernel(mine, first, count, where_ref, x_ref, *refs):
    odd = lax.rem(where_ref[0], 2)
    out_ref = refs[-1]
    for s in range(count):
        copy_rows(x_ref, odd if mine else 1 - odd, first + s, out_ref, s * 4 * x_ref.shape[3])


def take(where, x, mine, first, count, *after):
    return pl.pallas_call(
        functools.partial(take_kernel, mine, first, count),
        out_shape=jax.ShapeDtypeStruct((count * 4 * x.shape[3], SUBS, LANES), x.dtype),
        in_specs=[SMEM, VMEM] + [ANYWHERE] * len(after),
        out_specs=VMEM,
        compiler_params=params(),
        name="take",
    )(where, x, *after)


def take_extra_kernel(where_ref, x_ref, *refs):
    out_ref, turned = refs[-2:]
    odd = lax.rem(where_ref[0], 2)
    per_group, _, planes, cells = x_ref.shape[1:]
    layers = REACH - 1

    def fill(cloud, lowest):
        for s in range(per_group):
            copy_rows(x_ref, cloud, s, turned, 0)
            for k in range(4):
                out_ref[(4 * s + k) * layers : (4 * s + k + 1) * layers] = turned[k * planes + lowest : k * planes + lowest + layers]

    @pl.when(odd == 1)
    def _():
        fill(0, planes - layers)

    @pl.when(odd == 0)
    def _():
        fill(1, 0)


def take_extra(where, x, *after):
    per_group, _, planes, _ = x.shape[1:]
    return pl.pallas_call(
        take_extra_kernel,
        out_shape=jax.ShapeDtypeStruct((per_group * 4 * (REACH - 1), SUBS, LANES), x.dtype),
        in_specs=[SMEM, VMEM] + [ANYWHERE] * len(after),
        out_specs=VMEM,
        scratch_shapes=[pltpu.VMEM((4 * planes, SUBS, LANES), x.dtype)],
        compiler_params=params(),
        name="take_extra",
    )(where, x, *after)


def join_kernel(count, *refs):
    out_ref = refs[-1]
    first = 0
    for ref in refs[:count]:
        out_ref[first : first + ref.shape[0]] = ref[...]
        first += ref.shape[0]


def join(pieces, *after):
    rows = sum(piece.shape[0] for piece in pieces)
    return pl.pallas_call(
        functools.partial(join_kernel, len(pieces)),
        out_shape=jax.ShapeDtypeStruct((rows, *pieces[0].shape[1:]), pieces[0].dtype),
        in_specs=[VMEM] * len(pieces) + [ANYWHERE] * len(after),
        out_specs=VMEM,
        compiler_params=params(),
        name="join",
    )(*pieces, *after)


def total_kernel(count, where_ref, *refs):
    odd = lax.rem(where_ref[0], 2)
    mine_ref, other_ref = refs[-2:]
    total = refs[0][...]
    for ref in refs[1:count]:
        total = total + ref[...]
    mine_ref[...] = jnp.where(odd == 1, total[1], total[0])
    other_ref[...] = jnp.where(odd == 1, total[0], total[1])


def total_of(where, terms, *after):
    return pl.pallas_call(
        functools.partial(total_kernel, len(terms)),
        out_shape=[jax.ShapeDtypeStruct(terms[0].shape[1:], terms[0].dtype)] * 2,
        in_specs=[SMEM] + [VMEM] * len(terms) + [ANYWHERE] * len(after),
        out_specs=[VMEM] * 2,
        compiler_params=params(),
        name="total",
    )(where, *terms, *after)


def raw_density_kernel(x_ref, *refs):
    out_ref = refs[-1]
    clouds, states, _, planes, cells = x_ref.shape
    for j in range(clouds):
        for t in range(cells // LANES):
            lanes = pl.ds(t * LANES, LANES)
            sums = [jnp.zeros((planes, LANES), jnp.float32)] * 3
            for s in range(states):
                terms = densities(*[x_ref[j, s, k, :, lanes] for k in range(4)])
                sums = [a + b for a, b in zip(sums, terms)]
            for f in range(3):
                out_ref[j, f, :, lanes] = sums[f]


def raw_density(x, *after):
    clouds, _, _, planes, cells = x.shape
    return pl.pallas_call(
        raw_density_kernel,
        out_shape=jax.ShapeDtypeStruct((clouds, 3, planes, cells), jnp.float32),
        in_specs=[VMEM] + [ANYWHERE] * len(after),
        out_specs=VMEM,
        compiler_params=params(),
        name="raw_density",
    )(x, *after)


def slots_of(cloud):
    return [jnp.where(cloud == 0, q, 3 - q) for q in range(4)]


def first_layer(cloud, slot, slab, planes, shift_ref):
    return jnp.where(cloud == 0, (slab - 3 + slot) * planes + shift_ref[0], (slab + slot) * planes - shift_ref[1])


def window_start(cloud, planes, reach, shift_ref):
    return jnp.where(cloud == 0, 3 * planes - reach - shift_ref[0], shift_ref[1] - reach)


def placed_fields_kernel(depth, scale, where_ref, shift_ref, wave_ref, *refs):
    mine_refs, other_refs = refs[0:4], refs[4:8]
    out_ref, held = refs[-2:]
    planes, cells = mine_refs[0].shape[1:]
    slab = where_ref[0]
    odd = lax.rem(slab, 2)
    count = out_ref.shape[1]
    totals = [jnp.zeros((count, SUBS, LANES), jnp.float32)] * 3
    for cloud, slot_refs in ((odd, mine_refs), (1 - odd, other_refs)):
        for slot, ref in zip(slots_of(cloud), slot_refs):
            cos, sin = phase(2 * wave_ref[cloud], first_layer(cloud, slot, slab, planes, shift_ref), depth)
            layers = pl.ds(slot * planes, planes)
            for t in range(cells // LANES):
                lanes = pl.ds(t * LANES, LANES)
                kr, ki = ref[1, :, lanes], ref[2, :, lanes]
                held[0, layers, t, :] = ref[0, :, lanes]
                held[1, layers, t, :] = kr * cos - ki * sin
                held[2, layers, t, :] = kr * sin + ki * cos
        start = window_start(cloud, planes, HALO, shift_ref)
        totals = [total + held[f, pl.ds(start, count)] for f, total in enumerate(totals)]
    for f, field in enumerate(fields_of(*totals, scale)):
        out_ref[f] = field


def placed_fields(where, shift, wave, mine, other, depth, scale, *after):
    planes = mine[0].shape[1]
    return pl.pallas_call(
        functools.partial(placed_fields_kernel, depth, scale),
        out_shape=jax.ShapeDtypeStruct((3, planes + 2 * HALO, SUBS, LANES), jnp.float32),
        in_specs=[SMEM] * 3 + [VMEM] * 8 + [ANYWHERE] * len(after),
        out_specs=VMEM,
        scratch_shapes=[pltpu.VMEM((3, 4 * planes, SUBS, LANES), jnp.float32)],
        compiler_params=params(),
        name="placed_fields",
    )(where, shift, wave, *mine, *other, *after)


def transverse(x, weights):
    rows = x.shape[0]
    flat = x.reshape(rows * SUBS, LANES)
    high = flat.astype(jnp.bfloat16)
    low = (flat - high.astype(jnp.float32)).astype(jnp.bfloat16)
    product = jnp.dot(jnp.concatenate([high, low], axis=1), weights, preferred_element_type=jnp.float32)
    sub = lax.broadcasted_iota(jnp.int32, (rows * SUBS, LANES), 0) % SUBS
    up = pltpu.roll(product[:, :LANES].reshape(rows, SUBS, LANES), 1, 1).reshape(rows * SUBS, LANES)
    down = pltpu.roll(product[:, 2 * LANES :].reshape(rows, SUBS, LANES), SUBS - 1, 1).reshape(rows * SUBS, LANES)
    result = product[:, LANES : 2 * LANES] + jnp.where(sub > 0, up, 0.0) + jnp.where(sub < SUBS - 1, down, 0.0)
    return result.reshape(rows, SUBS, LANES)


def kinetic(layers, weights):
    count = layers.shape[1] - 2 * HALO
    inner = layers[:, HALO : HALO + count]
    along = stencil[0] * inner
    for j in range(1, HALO + 1):
        along = along + stencil[j] * (layers[:, HALO - j : HALO - j + count] + layers[:, HALO + j : HALO + j + count])
    across = transverse(inner.reshape(4 * count, SUBS, LANES), weights).reshape(inner.shape)
    return -0.5 * along + (-0.5 / 180.0) * across


def gather_kernel(depth, planes, mine, starts, where_ref, shift_ref, wave_ref, weights_ref, far_ref, second_ref, next_ref, own_ref, *refs):
    boosted_ref, base_ref, turns, window = refs[-4:]
    slab = where_ref[0]
    odd = lax.rem(slab, 2)
    cloud = odd if mine else 1 - odd
    states, _, count = boosted_ref.shape[:3]
    layers = REACH - 1
    far_edge = jnp.where(cloud == 0, planes - layers, 0)
    own_edge = jnp.where(cloud == 0, 0, planes - layers)
    slots = slots_of(cloud)
    for slot in slots:
        for n, part in enumerate(phase(wave_ref[cloud], first_layer(cloud, slot, slab, planes, shift_ref), depth)):
            for z in range(planes):
                turns[n, slot * planes + z] = jnp.broadcast_to(part[z : z + 1], (SUBS, LANES))
    start = window_start(cloud, planes, REACH, shift_ref)

    def one_state(s, _):
        def fill(place, ref, row, pitch, number):
            for n in range(number):
                cos, sin = turns[0, place + n], turns[1, place + n]
                u_re, u_im, v_re, v_im = [ref[row + k * pitch + n] for k in range(4)]
                window[0, place + n] = u_re * cos - u_im * sin
                window[1, place + n] = u_re * sin + u_im * cos
                window[2, place + n] = v_re * cos + v_im * sin
                window[3, place + n] = v_im * cos - v_re * sin

        rows = [(start + s) * 4 * planes for start in starts]
        if mine:
            fill(slots[0] * planes + far_edge, far_ref, (starts[0] + s) * 4 * layers, layers, layers)
        else:
            fill(slots[0] * planes + far_edge, far_ref, rows[0] + far_edge, planes, layers)
        fill(slots[1] * planes, second_ref, rows[1], planes, planes)
        fill(slots[2] * planes, next_ref, rows[2], planes, planes)
        fill(slots[3] * planes + own_edge, own_ref, rows[3] + own_edge, planes, layers)

        whole = window[:, pl.ds(start, count + 2 * HALO)]
        values = whole[:, HALO : HALO + count]
        kin = kinetic(whole, weights_ref[...])
        boosted_ref[s] = values
        base_ref[s, 0] = values[0] + time_step * kin[1]
        base_ref[s, 1] = values[1] - time_step * kin[0]
        base_ref[s, 2] = values[2] - time_step * kin[3]
        base_ref[s, 3] = values[3] + time_step * kin[2]
        return 0

    lax.fori_loop(0, states, one_state, 0)


def gather(where, shift, wave, weights, mine, pieces, count, planes, depth, *after):
    arrays, starts = zip(*pieces)
    shape = jax.ShapeDtypeStruct((count, 4, planes + 2 * HALO, SUBS, LANES), jnp.float32)
    return pl.pallas_call(
        functools.partial(gather_kernel, depth, planes, mine, starts),
        out_shape=[shape] * 2,
        in_specs=[SMEM] * 3 + [VMEM] * 5 + [ANYWHERE] * len(after),
        out_specs=[VMEM] * 2,
        scratch_shapes=[pltpu.VMEM((2, 4 * planes, SUBS, LANES), jnp.float32), pltpu.VMEM((4, 4 * planes, SUBS, LANES), jnp.float32)],
        compiler_params=params(),
        name="gather",
    )(where, shift, wave, weights, *arrays, *after)


def density_kernel(pieces, fields, *refs):
    boosted_refs, base_refs = refs[:pieces], refs[pieces : 2 * pieces]
    out_ref, sums = refs[2 * pieces :]
    planes = sums.shape[1]
    for z in range(planes):
        field = [fields[f, HALO + z] for f in range(3)]
        total = [jnp.zeros((SUBS, LANES), jnp.float32)] * 3
        for boosted, base in zip(boosted_refs, base_refs):
            for s in range(boosted.shape[0]):
                part = local_part(field, *[boosted[s, k, HALO + z] for k in range(4)])
                pr = base[s, 0, HALO + z] + time_step * part[1]
                pi = base[s, 1, HALO + z] - time_step * part[0]
                hr = base[s, 2, HALO + z] + time_step * part[3]
                hi = base[s, 3, HALO + z] - time_step * part[2]
                total = [a + b for a, b in zip(total, densities(pr, pi, hr, hi))]
        for f in range(3):
            sums[f, z] = total[f]
    for f in range(3):
        for t in range(SUBS):
            out_ref[f, :, t * LANES : (t + 1) * LANES] = sums[f, :, t, :]


def density(fields, boosted, base, planes):
    pieces = len(boosted)
    return pl.pallas_call(
        functools.partial(density_kernel, pieces),
        out_shape=jax.ShapeDtypeStruct((3, planes, SUBS * LANES), jnp.float32),
        in_specs=[VMEM] * (1 + 2 * pieces),
        out_specs=VMEM,
        scratch_shapes=[pltpu.VMEM((3, planes, SUBS, LANES), jnp.float32)],
        compiler_params=params(),
        name="density",
    )(fields, *boosted, *base)


def free_kernel(places, where_ref, weights_ref, fields, *refs):
    pieces = len(places)
    boosted_refs, base_refs = refs[:pieces], refs[pieces : 2 * pieces]
    free_ref, predicted_ref, window, turned = refs[2 * pieces :]
    planes = free_ref.shape[3]
    inner = pl.ds(HALO, planes)
    odd = lax.rem(where_ref[0], 2)
    for (mine, first, count), boosted, base in zip(places, boosted_refs, base_refs):
        j = odd if mine else 1 - odd

        def one_state(s, _):
            for z in range(planes + 2 * HALO):
                field = [fields[f, z] for f in range(3)]
                part = local_part(field, *[boosted[s, k, z] for k in range(4)])
                window[0, z] = base[s, 0, z] + time_step * part[1]
                window[1, z] = base[s, 1, z] - time_step * part[0]
                window[2, z] = base[s, 2, z] + time_step * part[3]
                window[3, z] = base[s, 3, z] - time_step * part[2]
            kin = kinetic(window[...], weights_ref[...])
            mean = [0.5 * (boosted[s, k, inner] + window[k, inner]) for k in range(4)]
            half = 0.5 * time_step
            turned[0] = mean[0] + half * kin[1]
            turned[1] = mean[1] - half * kin[0]
            turned[2] = mean[2] - half * kin[3]
            turned[3] = mean[3] + half * kin[2]
            for k in range(4):
                for t in range(SUBS):
                    lanes = pl.ds(t * LANES, LANES)
                    free_ref[j, first + s, k, :, lanes] = turned[k, :, t, :]
                    predicted_ref[j, first + s, k, :, lanes] = window[k, inner, t, :]
            return 0

        lax.fori_loop(0, count, one_state, 0)


def free_part(where, weights, fields, boosted, base, places, shape, planes):
    pieces = len(places)
    out = jax.ShapeDtypeStruct(shape, jnp.float32)
    return pl.pallas_call(
        functools.partial(free_kernel, places),
        out_shape=[out] * 2,
        in_specs=[SMEM] + [VMEM] * (2 + 2 * pieces),
        out_specs=[VMEM] * 2,
        scratch_shapes=[
            pltpu.VMEM((4, planes + 2 * HALO, SUBS, LANES), jnp.float32),
            pltpu.VMEM((4, planes, SUBS, LANES), jnp.float32),
        ],
        compiler_params=params(),
        name="free_part",
    )(where, weights, fields, *boosted, *base)


def last_kernel(scale, *refs):
    partial_refs = refs[:-4]
    free_ref, predicted_ref, out_ref, fields = refs[-4:]

    @pl.when(pl.program_id(0) == 0)
    def _():
        totals = []
        for f in range(3):
            total = partial_refs[0][f]
            for ref in partial_refs[1:]:
                total = total + ref[f]
            totals.append(total)
        for f, field in enumerate(fields_of(*totals, scale)):
            fields[f] = field

    half = 0.5 * time_step
    for t in range(free_ref.shape[-1] // LANES):
        lanes = pl.ds(t * LANES, LANES)
        field = [fields[f, :, lanes] for f in range(3)]
        for s in range(free_ref.shape[1]):
            part = local_part(field, *[predicted_ref[0, s, k, :, lanes] for k in range(4)])
            out_ref[0, s, 0, :, lanes] = free_ref[0, s, 0, :, lanes] + half * part[1]
            out_ref[0, s, 1, :, lanes] = free_ref[0, s, 1, :, lanes] - half * part[0]
            out_ref[0, s, 2, :, lanes] = free_ref[0, s, 2, :, lanes] + half * part[3]
            out_ref[0, s, 3, :, lanes] = free_ref[0, s, 3, :, lanes] - half * part[2]


def last_part(partials, free, predicted, scale):
    shape = free.shape
    whole = pl.BlockSpec(partials[0].shape, lambda i: (0, 0, 0))
    block = pl.BlockSpec((1, *shape[1:]), lambda i: (i, 0, 0, 0, 0))
    return pl.pallas_call(
        functools.partial(last_kernel, scale),
        out_shape=jax.ShapeDtypeStruct(shape, jnp.float32),
        grid=(shape[0],),
        in_specs=[whole] * len(partials) + [block] * 2,
        out_specs=block,
        scratch_shapes=[pltpu.VMEM(partials[0].shape, jnp.float32)],
        compiler_params=params(),
        name="last_part",
    )(*partials, free, predicted)


def local(weights, cloud_states, cloud_shift, boost_wave):
    slab_count, group_count = lax.axis_size("slab"), lax.axis_size("grp")
    _, per_group, _, planes, cells = cloud_states.shape
    depth = planes * slab_count
    scale = 1.0 / (per_group * group_count)
    where = lax.axis_index("slab").astype(jnp.int32).reshape(1)

    even_on = lambda a: lax.ppermute(a, "slab", [(i, (i - 2 if i % 2 else i + 2) % slab_count) for i in range(slab_count)])
    odd_on = lambda a: lax.ppermute(a, "slab", [(i, (i + 2 if i % 2 else i - 2) % slab_count) for i in range(slab_count)])
    across = lambda a: lax.ppermute(a, "slab", [(i, (i + 3 if i % 2 else i - 3) % slab_count) for i in range(slab_count)])

    def group_terms(a):
        if group_count > 4:
            return [lax.psum(a, "grp")]
        return [a] + [moved(a, "grp", d) for d in range(1, group_count)]

    chunks = [(0, per_group)]
    mine = [take(where, cloud_states, True, *chunk) for chunk in chunks]
    mine_second = [even_on(piece) for piece in mine]
    other = [take(where, cloud_states, False, *chunk) for chunk in chunks]
    other_second = [odd_on(piece) for piece in other]
    terms = group_terms(raw_density(cloud_states, *mine, *other))
    mine_sums, other_sums = total_of(where, terms, *mine_second)
    extra = across(take_extra(where, cloud_states, mine[0]))

    mine_sums_second, other_sums_second, far_sums = even_on(mine_sums), odd_on(other_sums), across(other_sums)
    other_next = swapped(mine[0])
    other_far = swapped(mine_second[0])
    joined = join([mine_sums_second, other_sums_second, mine_sums], extra, far_sums)
    swapped_sums = swapped(joined)
    swapped_sums = [swapped_sums[3 * n : 3 * n + 3] for n in range(3)]
    mine_next = [swapped(piece) for piece in other_second]
    work = lambda *a: gather(where, cloud_shift, boost_wave, weights, *a, planes, depth)
    places, worked = [], []
    for n, (first, count) in enumerate(chunks):
        worked.append(work(False, [(other_far, first), (other_second[n], 0), (other_next, first), (other[n], 0)], count))
        places.append((False, first, count))
    fields = placed_fields(
        where, cloud_shift, boost_wave, [far_sums, mine_sums_second, swapped_sums[1], mine_sums],
        [swapped_sums[0], other_sums_second, swapped_sums[2], other_sums], depth, scale, *[piece[0] for piece in worked],
    )
    for n, (first, count) in enumerate(chunks):
        worked.append(work(True, [(extra, first), (mine_second[n], 0), (mine_next[n], 0), (mine[n], 0)], count))
        places.append((True, first, count))
    boosted, base = [list(part) for part in zip(*worked)]
    partials = group_terms(density(fields, boosted, base, planes))
    free, predicted = free_part(where, weights, fields, boosted, base, tuple(places), cloud_states.shape, planes)
    return last_part(partials, free, predicted, scale)


def solution(mesh):
    states = P(None, "grp", None, "slab", None)
    weights = transverse_weights()
    step = jax.shard_map(local, mesh=mesh, in_specs=(P(), states, P(), P()), out_specs=states, check_vma=False)
    return lambda cloud_states, cloud_shift, boost_wave: step(weights, cloud_states, cloud_shift, boost_wave)
```

```python
import functools
import math

import jax
import jax.numpy as jnp
import numpy as np
from jax import lax
from jax.experimental import pallas as pl
from jax.experimental.pallas import tpu as pltpu
from jax.sharding import PartitionSpec as P

NY = 32
LANES = 128
SUBS = 8
HALO = 3
REACH = 2 * HALO
VMEM_BYTES = 40 * 1024 * 1024

stencil = (-49.0 / 18.0, 1.5, -0.15, 1.0 / 90.0)
coupling = 3.0
xi_factor = 1.2
chemical = 1.0
time_step = 0.1

VMEM = pl.BlockSpec(memory_space=pltpu.VMEM)
SMEM = pl.BlockSpec(memory_space=pltpu.SMEM)
ANYWHERE = pl.BlockSpec(memory_space=pl.ANY)


def params():
    return pltpu.CompilerParams(vmem_limit_bytes=VMEM_BYTES)


def moved(x, axis, by):
    peers = lax.axis_size(axis)
    return lax.ppermute(x, axis, [(i, (i + by) % peers) for i in range(peers)])


def swapped(x):
    peers = lax.axis_size("slab")
    return lax.ppermute(x, "slab", [(i, i ^ 1) for i in range(peers)])


def transverse_weights():
    whole = {0: -980.0, 1: 270.0, 2: -27.0, 3: 2.0}
    rows = LANES // NY
    weights = np.zeros((LANES, 3 * LANES), np.float32)
    for a in range(LANES):
        xa, ya = divmod(a, NY)
        for b in range(LANES):
            xb, yb = divmod(b, NY)
            for part, distance in ((0, xb + rows - xa), (1, xb - xa), (2, xb - rows - xa)):
                if ya == yb and abs(distance) <= HALO:
                    weights[a, part * LANES + b] += whole[abs(distance)]
            if xa == xb and 0 < abs(ya - yb) <= HALO:
                weights[a, LANES + b] += whole[abs(ya - yb)]
    return np.concatenate([weights, weights]).astype(jnp.bfloat16)


def phase(wave, first, depth):
    z = first + lax.broadcasted_iota(jnp.int32, (SUBS, LANES), 0)
    index = jnp.bitwise_and(wave * z, depth - 1)
    angle = (2.0 * math.pi / depth) * index.astype(jnp.float32)
    return jnp.cos(angle), jnp.sin(angle)


def densities(ur, ui, vr, vi):
    return vr * vr + vi * vi, ur * vr + ui * vi, ui * vr - ur * vi


def fields_of(n, kr, ki, scale):
    n = n * scale
    safe = jnp.where(n > 0.0, n, 1.0)
    power = jnp.where(n > 0.0, jnp.exp((2.0 / 3.0) * jnp.log(safe)), 0.0)
    return xi_factor * power - chemical, (-coupling * scale) * kr, (-coupling * scale) * ki


def local_part(field, ur, ui, vr, vi):
    potential, gap_real, gap_imag = field
    return (
        potential * ur + gap_real * vr - gap_imag * vi,
        potential * ui + gap_real * vi + gap_imag * vr,
        gap_real * ur + gap_imag * ui - potential * vr,
        gap_real * ui - gap_imag * ur - potential * vi,
    )


def copy_rows(x_ref, cloud, state, out_ref, first_row):
    planes, cells = x_ref.shape[3:]
    for k in range(4):
        rows = pl.ds(first_row + k * planes, planes)
        for t in range(cells // LANES):
            out_ref[rows, t, :] = x_ref[cloud, state, k, :, t * LANES : (t + 1) * LANES]


def take_kernel(mine, first, count, where_ref, x_ref, *refs):
    odd = lax.rem(where_ref[0], 2)
    out_ref = refs[-1]
    for s in range(count):
        copy_rows(x_ref, odd if mine else 1 - odd, first + s, out_ref, s * 4 * x_ref.shape[3])


def take(where, x, mine, first, count, *after):
    return pl.pallas_call(
        functools.partial(take_kernel, mine, first, count),
        out_shape=jax.ShapeDtypeStruct((count * 4 * x.shape[3], SUBS, LANES), x.dtype),
        in_specs=[SMEM, VMEM] + [ANYWHERE] * len(after),
        out_specs=VMEM,
        compiler_params=params(),
        name="take",
    )(where, x, *after)


def take_extra_kernel(where_ref, x_ref, *refs):
    out_ref, turned = refs[-2:]
    odd = lax.rem(where_ref[0], 2)
    per_group, _, planes, cells = x_ref.shape[1:]
    layers = REACH - 1

    def fill(cloud, lowest):
        for s in range(per_group):
            copy_rows(x_ref, cloud, s, turned, 0)
            for k in range(4):
                out_ref[(4 * s + k) * layers : (4 * s + k + 1) * layers] = turned[k * planes + lowest : k * planes + lowest + layers]

    @pl.when(odd == 1)
    def _():
        fill(0, planes - layers)

    @pl.when(odd == 0)
    def _():
        fill(1, 0)


def take_extra(where, x, *after):
    per_group, _, planes, _ = x.shape[1:]
    return pl.pallas_call(
        take_extra_kernel,
        out_shape=jax.ShapeDtypeStruct((per_group * 4 * (REACH - 1), SUBS, LANES), x.dtype),
        in_specs=[SMEM, VMEM] + [ANYWHERE] * len(after),
        out_specs=VMEM,
        scratch_shapes=[pltpu.VMEM((4 * planes, SUBS, LANES), x.dtype)],
        compiler_params=params(),
        name="take_extra",
    )(where, x, *after)


def join_kernel(count, *refs):
    out_ref = refs[-1]
    first = 0
    for ref in refs[:count]:
        out_ref[first : first + ref.shape[0]] = ref[...]
        first += ref.shape[0]


def join(pieces, *after):
    rows = sum(piece.shape[0] for piece in pieces)
    return pl.pallas_call(
        functools.partial(join_kernel, len(pieces)),
        out_shape=jax.ShapeDtypeStruct((rows, *pieces[0].shape[1:]), pieces[0].dtype),
        in_specs=[VMEM] * len(pieces) + [ANYWHERE] * len(after),
        out_specs=VMEM,
        compiler_params=params(),
        name="join",
    )(*pieces, *after)


def add_kernel(a_ref, b_ref, *refs):
    refs[-1][...] = a_ref[...] + b_ref[...]


def add(a, b, *after):
    return pl.pallas_call(
        add_kernel,
        out_shape=jax.ShapeDtypeStruct(a.shape, a.dtype),
        in_specs=[VMEM] * 2 + [ANYWHERE] * len(after),
        out_specs=VMEM,
        compiler_params=params(),
        name="add",
    )(a, b, *after)


def total_kernel(count, where_ref, *refs):
    odd = lax.rem(where_ref[0], 2)
    mine_ref, other_ref = refs[-2:]
    total = refs[0][...]
    for ref in refs[1:count]:
        total = total + ref[...]
    mine_ref[...] = jnp.where(odd == 1, total[1], total[0])
    other_ref[...] = jnp.where(odd == 1, total[0], total[1])


def total_of(where, terms, *after):
    return pl.pallas_call(
        functools.partial(total_kernel, len(terms)),
        out_shape=[jax.ShapeDtypeStruct(terms[0].shape[1:], terms[0].dtype)] * 2,
        in_specs=[SMEM] + [VMEM] * len(terms) + [ANYWHERE] * len(after),
        out_specs=[VMEM] * 2,
        compiler_params=params(),
        name="total",
    )(where, *terms, *after)


def raw_density_kernel(x_ref, *refs):
    out_ref = refs[-1]
    clouds, states, _, planes, cells = x_ref.shape
    for j in range(clouds):
        for t in range(cells // LANES):
            lanes = pl.ds(t * LANES, LANES)
            sums = [jnp.zeros((planes, LANES), jnp.float32)] * 3
            for s in range(states):
                terms = densities(*[x_ref[j, s, k, :, lanes] for k in range(4)])
                sums = [a + b for a, b in zip(sums, terms)]
            for f in range(3):
                out_ref[j, f, :, lanes] = sums[f]


def raw_density(x, *after):
    clouds, _, _, planes, cells = x.shape
    return pl.pallas_call(
        raw_density_kernel,
        out_shape=jax.ShapeDtypeStruct((clouds, 3, planes, cells), jnp.float32),
        in_specs=[VMEM] + [ANYWHERE] * len(after),
        out_specs=VMEM,
        compiler_params=params(),
        name="raw_density",
    )(x, *after)


def slots_of(cloud):
    return [jnp.where(cloud == 0, q, 3 - q) for q in range(4)]


def first_layer(cloud, slot, slab, planes, shift_ref):
    return jnp.where(cloud == 0, (slab - 3 + slot) * planes + shift_ref[0], (slab + slot) * planes - shift_ref[1])


def window_start(cloud, planes, reach, shift_ref):
    return jnp.where(cloud == 0, 3 * planes - reach - shift_ref[0], shift_ref[1] - reach)


def placed_fields_kernel(depth, scale, where_ref, shift_ref, wave_ref, *refs):
    mine_refs, other_refs = refs[0:4], refs[4:8]
    out_ref, held = refs[-2:]
    planes, cells = mine_refs[0].shape[1:]
    slab = where_ref[0]
    odd = lax.rem(slab, 2)
    count = out_ref.shape[1]
    totals = [jnp.zeros((count, SUBS, LANES), jnp.float32)] * 3
    for cloud, slot_refs in ((odd, mine_refs), (1 - odd, other_refs)):
        for slot, ref in zip(slots_of(cloud), slot_refs):
            cos, sin = phase(2 * wave_ref[cloud], first_layer(cloud, slot, slab, planes, shift_ref), depth)
            layers = pl.ds(slot * planes, planes)
            for t in range(cells // LANES):
                lanes = pl.ds(t * LANES, LANES)
                kr, ki = ref[1, :, lanes], ref[2, :, lanes]
                held[0, layers, t, :] = ref[0, :, lanes]
                held[1, layers, t, :] = kr * cos - ki * sin
                held[2, layers, t, :] = kr * sin + ki * cos
        start = window_start(cloud, planes, HALO, shift_ref)
        totals = [total + held[f, pl.ds(start, count)] for f, total in enumerate(totals)]
    for f, field in enumerate(fields_of(*totals, scale)):
        out_ref[f] = field


def placed_fields(where, shift, wave, mine, other, depth, scale, *after):
    planes = mine[0].shape[1]
    return pl.pallas_call(
        functools.partial(placed_fields_kernel, depth, scale),
        out_shape=jax.ShapeDtypeStruct((3, planes + 2 * HALO, SUBS, LANES), jnp.float32),
        in_specs=[SMEM] * 3 + [VMEM] * 8 + [ANYWHERE] * len(after),
        out_specs=VMEM,
        scratch_shapes=[pltpu.VMEM((3, 4 * planes, SUBS, LANES), jnp.float32)],
        compiler_params=params(),
        name="placed_fields",
    )(where, shift, wave, *mine, *other, *after)


def transverse(x, weights):
    rows = x.shape[0]
    flat = x.reshape(rows * SUBS, LANES)
    high = flat.astype(jnp.bfloat16)
    low = (flat - high.astype(jnp.float32)).astype(jnp.bfloat16)
    product = jnp.dot(jnp.concatenate([high, low], axis=1), weights, preferred_element_type=jnp.float32)
    sub = lax.broadcasted_iota(jnp.int32, (rows * SUBS, LANES), 0) % SUBS
    up = pltpu.roll(product[:, :LANES].reshape(rows, SUBS, LANES), 1, 1).reshape(rows * SUBS, LANES)
    down = pltpu.roll(product[:, 2 * LANES :].reshape(rows, SUBS, LANES), SUBS - 1, 1).reshape(rows * SUBS, LANES)
    result = product[:, LANES : 2 * LANES] + jnp.where(sub > 0, up, 0.0) + jnp.where(sub < SUBS - 1, down, 0.0)
    return result.reshape(rows, SUBS, LANES)


def kinetic(layers, weights):
    count = layers.shape[1] - 2 * HALO
    inner = layers[:, HALO : HALO + count]
    along = stencil[0] * inner
    for j in range(1, HALO + 1):
        along = along + stencil[j] * (layers[:, HALO - j : HALO - j + count] + layers[:, HALO + j : HALO + j + count])
    across = transverse(inner.reshape(-1, SUBS, LANES), weights).reshape(inner.shape)
    return -0.5 * along + (-0.5 / 180.0) * across


def turned(u_re, u_im, v_re, v_im, cos, sin):
    return u_re * cos - u_im * sin, u_re * sin + u_im * cos, v_re * cos + v_im * sin, v_im * cos - v_re * sin


def gather_kernel(depth, planes, mine, starts, where_ref, shift_ref, wave_ref, weights_ref, far_ref, second_ref, next_ref, own_ref, *refs):
    windows, boosted_ref, base_ref, turns = refs[-4:]
    slab = where_ref[0]
    odd = lax.rem(slab, 2)
    cloud = odd if mine else 1 - odd
    states, _, count = boosted_ref.shape[:3]
    layers = REACH - 1
    far_edge = jnp.where(cloud == 0, planes - layers, 0)
    own_edge = jnp.where(cloud == 0, 0, planes - layers)
    slots = slots_of(cloud)
    for slot in slots:
        for n, part in enumerate(phase(wave_ref[cloud], first_layer(cloud, slot, slab, planes, shift_ref), depth)):
            for z in range(planes):
                turns[n, slot * planes + z] = jnp.broadcast_to(part[z : z + 1], (SUBS, LANES))
    start = window_start(cloud, planes, HALO, shift_ref)

    for s in range(states):
        def fill(place, ref, row, pitch, number):
            for n in range(number):
                parts = [ref[row + k * pitch + n] for k in range(4)]
                for k, value in enumerate(turned(*parts, turns[0, place + n], turns[1, place + n])):
                    windows[s, k, place + n] = value

        rows = [(start_state + s) * 4 * planes for start_state in starts]
        if mine:
            fill(slots[0] * planes + far_edge, far_ref, (starts[0] + s) * 4 * layers, layers, layers)
        else:
            fill(slots[0] * planes + far_edge, far_ref, rows[0] + far_edge, planes, layers)
        fill(slots[1] * planes, second_ref, rows[1], planes, planes)
        fill(slots[2] * planes, next_ref, rows[2], planes, planes)
        fill(slots[3] * planes + own_edge, own_ref, rows[3] + own_edge, planes, layers)

        whole = windows[s, :, pl.ds(start, count + 2 * HALO)]
        values = whole[:, HALO : HALO + count]
        kin = kinetic(whole, weights_ref[...])
        boosted_ref[s] = values
        base_ref[s, 0] = values[0] + time_step * kin[1]
        base_ref[s, 1] = values[1] - time_step * kin[0]
        base_ref[s, 2] = values[2] - time_step * kin[3]
        base_ref[s, 3] = values[3] + time_step * kin[2]


def gather(where, shift, wave, weights, mine, pieces, count, planes, depth, *after):
    arrays, starts = zip(*pieces)
    shapes = [(count, 4, 4 * planes, SUBS, LANES)] + [(count, 4, planes, SUBS, LANES)] * 2
    return pl.pallas_call(
        functools.partial(gather_kernel, depth, planes, mine, starts),
        out_shape=[jax.ShapeDtypeStruct(shape, jnp.float32) for shape in shapes],
        in_specs=[SMEM] * 3 + [VMEM] * 5 + [ANYWHERE] * len(after),
        out_specs=[VMEM] * 3,
        scratch_shapes=[pltpu.VMEM((2, 4 * planes, SUBS, LANES), jnp.float32)],
        compiler_params=params(),
        name="gather",
    )(where, shift, wave, weights, *arrays, *after)


def density_kernel(pieces, fields, *refs):
    boosted_refs, base_refs = refs[:pieces], refs[pieces : 2 * pieces]
    out_ref, sums = refs[2 * pieces :]
    planes = sums.shape[1]
    for z in range(planes):
        field = [fields[f, HALO + z] for f in range(3)]
        total = [jnp.zeros((SUBS, LANES), jnp.float32)] * 3
        for boosted, base in zip(boosted_refs, base_refs):
            for s in range(boosted.shape[0]):
                part = local_part(field, *[boosted[s, k, z] for k in range(4)])
                pr = base[s, 0, z] + time_step * part[1]
                pi = base[s, 1, z] - time_step * part[0]
                hr = base[s, 2, z] + time_step * part[3]
                hi = base[s, 3, z] - time_step * part[2]
                total = [a + b for a, b in zip(total, densities(pr, pi, hr, hi))]
        for f in range(3):
            sums[f, z] = total[f]
    for f in range(3):
        for t in range(SUBS):
            out_ref[f, :, t * LANES : (t + 1) * LANES] = sums[f, :, t, :]


def density(fields, boosted, base, planes):
    pieces = len(boosted)
    return pl.pallas_call(
        functools.partial(density_kernel, pieces),
        out_shape=jax.ShapeDtypeStruct((3, planes, SUBS * LANES), jnp.float32),
        in_specs=[VMEM] * (1 + 2 * pieces),
        out_specs=VMEM,
        scratch_shapes=[pltpu.VMEM((3, planes, SUBS, LANES), jnp.float32)],
        compiler_params=params(),
        name="density",
    )(fields, *boosted, *base)


def free_kernel(places, where_ref, shift_ref, weights_ref, fields, *refs):
    pieces = len(places)
    windows, boosted_refs, base_refs = refs[:pieces], refs[pieces : 2 * pieces], refs[2 * pieces : 3 * pieces]
    free_ref, predicted_ref, window, combined = refs[3 * pieces :]
    planes = free_ref.shape[3]
    inner = pl.ds(HALO, planes)
    slab = where_ref[0]
    odd = lax.rem(slab, 2)
    edge = HALO + planes

    def predict(layer, field, boosted, base):
        part = local_part(field, *boosted)
        window[0, layer] = base[0] + time_step * part[1]
        window[1, layer] = base[1] - time_step * part[0]
        window[2, layer] = base[2] + time_step * part[3]
        window[3, layer] = base[3] - time_step * part[2]

    for (mine, first, count), boosted_window, boosted, base in zip(places, windows, boosted_refs, base_refs):
        j = odd if mine else 1 - odd
        start = window_start(j, planes, REACH, shift_ref)

        def one_state(s, _):
            sides = [boosted_window[s, :, pl.ds(start + first_side, 3 * HALO)] for first_side in (0, planes + HALO)]
            sides = jnp.concatenate(sides, axis=0)
            kin = kinetic(sides, weights_ref[...])
            for side, offset in ((0, 0), (1, edge)):
                for n in range(HALO):
                    value = [sides[4 * side + k, HALO + n] for k in range(4)]
                    turn = [kin[4 * side + k, n] for k in range(4)]
                    moved_on = [
                        value[0] + time_step * turn[1],
                        value[1] - time_step * turn[0],
                        value[2] - time_step * turn[3],
                        value[3] + time_step * turn[2],
                    ]
                    predict(offset + n, [fields[f, offset + n] for f in range(3)], value, moved_on)
            for z in range(planes):
                field = [fields[f, HALO + z] for f in range(3)]
                predict(HALO + z, field, [boosted[s, k, z] for k in range(4)], [base[s, k, z] for k in range(4)])
            kin = kinetic(window[...], weights_ref[...])
            mean = [0.5 * (boosted[s, k] + window[k, inner]) for k in range(4)]
            half = 0.5 * time_step
            combined[0] = mean[0] + half * kin[1]
            combined[1] = mean[1] - half * kin[0]
            combined[2] = mean[2] - half * kin[3]
            combined[3] = mean[3] + half * kin[2]
            for k in range(4):
                for t in range(SUBS):
                    lanes = pl.ds(t * LANES, LANES)
                    free_ref[0, first + s, k, :, lanes] = combined[k, :, t, :]
                    predicted_ref[0, first + s, k, :, lanes] = window[k, inner, t, :]
            return 0

        lax.fori_loop(0, count, one_state, 0)


def free_part(where, shift, weights, fields, windows, boosted, base, places, shape, planes):
    pieces = len(places)
    out = jax.ShapeDtypeStruct(shape, jnp.float32)
    return pl.pallas_call(
        functools.partial(free_kernel, tuple(places)),
        out_shape=[out] * 2,
        in_specs=[SMEM] * 2 + [VMEM] * (2 + 3 * pieces),
        out_specs=[VMEM] * 2,
        scratch_shapes=[
            pltpu.VMEM((4, planes + 2 * HALO, SUBS, LANES), jnp.float32),
            pltpu.VMEM((4, planes, SUBS, LANES), jnp.float32),
        ],
        compiler_params=params(),
        name="free_part",
    )(where, shift, weights, fields, *windows, *boosted, *base)


def last_kernel(scale, where_ref, *refs):
    partial_refs, pieces = refs[:-6], refs[-6:-2]
    out_ref, fields = refs[-2:]

    @pl.when(pl.program_id(0) == 0)
    def _():
        totals = []
        for f in range(3):
            total = partial_refs[0][f]
            for ref in partial_refs[1:]:
                total = total + ref[f]
            totals.append(total)
        for f, field in enumerate(fields_of(*totals, scale)):
            fields[f] = field

    half = 0.5 * time_step

    def write(free_ref, predicted_ref):
        for t in range(out_ref.shape[-1] // LANES):
            lanes = pl.ds(t * LANES, LANES)
            field = [fields[f, :, lanes] for f in range(3)]
            for s in range(out_ref.shape[1]):
                part = local_part(field, *[predicted_ref[0, s, k, :, lanes] for k in range(4)])
                out_ref[0, s, 0, :, lanes] = free_ref[0, s, 0, :, lanes] + half * part[1]
                out_ref[0, s, 1, :, lanes] = free_ref[0, s, 1, :, lanes] - half * part[0]
                out_ref[0, s, 2, :, lanes] = free_ref[0, s, 2, :, lanes] + half * part[3]
                out_ref[0, s, 3, :, lanes] = free_ref[0, s, 3, :, lanes] - half * part[2]

    mine = pl.program_id(0) == lax.rem(where_ref[0], 2)

    @pl.when(jnp.logical_not(mine))
    def _():
        write(pieces[0], pieces[2])

    @pl.when(mine)
    def _():
        write(pieces[1], pieces[3])


def last_part(where, partials, free, predicted, scale):
    shape = (2, *free[0].shape[1:])
    whole = lambda a: pl.BlockSpec(a.shape, lambda i: (0,) * a.ndim)
    return pl.pallas_call(
        functools.partial(last_kernel, scale),
        out_shape=jax.ShapeDtypeStruct(shape, jnp.float32),
        grid=(2,),
        in_specs=[SMEM] + [whole(a) for a in (*partials, *free, *predicted)],
        out_specs=pl.BlockSpec((1, *shape[1:]), lambda i: (i, 0, 0, 0, 0)),
        scratch_shapes=[pltpu.VMEM(partials[0].shape, jnp.float32)],
        compiler_params=params(),
        name="last_part",
    )(where, *partials, *free, *predicted)


def local(weights, cloud_states, cloud_shift, boost_wave):
    slab_count, group_count = lax.axis_size("slab"), lax.axis_size("grp")
    _, per_group, _, planes, cells = cloud_states.shape
    depth = planes * slab_count
    scale = 1.0 / (per_group * group_count)
    where = lax.axis_index("slab").astype(jnp.int32).reshape(1)

    even_on = lambda a: lax.ppermute(a, "slab", [(i, (i - 2 if i % 2 else i + 2) % slab_count) for i in range(slab_count)])
    odd_on = lambda a: lax.ppermute(a, "slab", [(i, (i + 2 if i % 2 else i - 2) % slab_count) for i in range(slab_count)])
    across = lambda a: lax.ppermute(a, "slab", [(i, (i + 3 if i % 2 else i - 3) % slab_count) for i in range(slab_count)])

    def paired(a, bit):
        return lax.ppermute(a, "grp", [(i, i ^ bit) for i in range(group_count)])

    def two_terms(a, *after):
        if group_count != 4:
            a = lax.psum(a, "grp")
            return [a, jnp.zeros_like(a)]
        a = add(a, paired(a, 1), *after)
        return [a, paired(a, 2)]

    def group_terms(a):
        if group_count > 4:
            return [lax.psum(a, "grp")]
        return [a] + [moved(a, "grp", d) for d in range(1, group_count)]

    chunks = [(0, per_group)]
    mine = [take(where, cloud_states, True, *chunk) for chunk in chunks]
    mine_second = [even_on(piece) for piece in mine]
    other = [take(where, cloud_states, False, *chunk) for chunk in chunks]
    other_second = [odd_on(piece) for piece in other]
    terms = two_terms(raw_density(cloud_states, *mine, *other))
    extra = across(take_extra(where, cloud_states, mine[0]))
    mine_sums, other_sums = total_of(where, terms, *mine_second, extra)

    mine_sums_second, other_sums_second, far_sums = even_on(mine_sums), odd_on(other_sums), across(other_sums)
    other_next = swapped(mine[0])
    other_far = swapped(join(mine_second, mine_sums))
    work = lambda *a: gather(where, cloud_shift, boost_wave, weights, *a, planes, depth)
    places, worked = [], []
    for n, (first, count) in enumerate(chunks):
        worked.append(work(False, [(other_far, first), (other_second[n], 0), (other_next, first), (other[n], 0)], count))
        places.append((False, first, count))
    joined = join([mine_sums_second, other_sums_second, mine_sums], far_sums, *[piece[1] for piece in worked])
    swapped_sums = swapped(joined)
    swapped_sums = [swapped_sums[3 * n : 3 * n + 3] for n in range(3)]
    mine_next = [swapped(join([piece], joined)) for piece in other_second]
    fields = placed_fields(
        where, cloud_shift, boost_wave, [far_sums, mine_sums_second, swapped_sums[1], mine_sums],
        [swapped_sums[0], other_sums_second, swapped_sums[2], other_sums], depth, scale,
    )
    for n, (first, count) in enumerate(chunks):
        worked.append(work(True, [(extra, first), (mine_second[n], 0), (mine_next[n], 0), (mine[n], 0)], count))
        places.append((True, first, count))
    windows, boosted, base = [list(part) for part in zip(*worked)]
    def free_of(n):
        return free_part(
            where, cloud_shift, weights, fields, windows[n : n + 1], boosted[n : n + 1], base[n : n + 1], places[n : n + 1],
            (1, *cloud_states.shape[1:]), planes,
        )

    first_parts = free_of(0)
    partials = two_terms(density(fields, boosted, base, planes), first_parts[0])
    free, predicted = zip(first_parts, free_of(1))
    return last_part(where, partials, free, predicted, scale)


def solution(mesh):
    states = P(None, "grp", None, "slab", None)
    weights = transverse_weights()
    step = jax.shard_map(local, mesh=mesh, in_specs=(P(), states, P(), P()), out_specs=states, check_vma=False)
    return lambda cloud_states, cloud_shift, boost_wave: step(weights, cloud_states, cloud_shift, boost_wave)
```

```python
import functools
import math

import jax
import jax.numpy as jnp
import numpy as np
from jax import lax
from jax.experimental import pallas as pl
from jax.experimental.pallas import tpu as pltpu
from jax.sharding import PartitionSpec as P

NY = 32
LANES = 128
SUBS = 8
HALO = 3
REACH = 2 * HALO
VMEM_BYTES = 40 * 1024 * 1024

stencil = (-49.0 / 18.0, 1.5, -0.15, 1.0 / 90.0)
coupling = 3.0
xi_factor = 1.2
chemical = 1.0
time_step = 0.1

VMEM = pl.BlockSpec(memory_space=pltpu.VMEM)
SMEM = pl.BlockSpec(memory_space=pltpu.SMEM)
ANYWHERE = pl.BlockSpec(memory_space=pl.ANY)


def params():
    return pltpu.CompilerParams(vmem_limit_bytes=VMEM_BYTES)


def moved(x, axis, by):
    peers = lax.axis_size(axis)
    return lax.ppermute(x, axis, [(i, (i + by) % peers) for i in range(peers)])


def swapped(x):
    peers = lax.axis_size("slab")
    return lax.ppermute(x, "slab", [(i, i ^ 1) for i in range(peers)])


def transverse_weights():
    whole = {0: -980.0, 1: 270.0, 2: -27.0, 3: 2.0}
    rows = LANES // NY
    weights = np.zeros((LANES, 3 * LANES), np.float32)
    for a in range(LANES):
        xa, ya = divmod(a, NY)
        for b in range(LANES):
            xb, yb = divmod(b, NY)
            for part, distance in ((0, xb + rows - xa), (1, xb - xa), (2, xb - rows - xa)):
                if ya == yb and abs(distance) <= HALO:
                    weights[a, part * LANES + b] += whole[abs(distance)]
            if xa == xb and 0 < abs(ya - yb) <= HALO:
                weights[a, LANES + b] += whole[abs(ya - yb)]
    return np.concatenate([weights, weights]).astype(jnp.bfloat16)


def phase(wave, first, depth):
    z = first + lax.broadcasted_iota(jnp.int32, (SUBS, LANES), 0)
    index = jnp.bitwise_and(wave * z, depth - 1)
    angle = (2.0 * math.pi / depth) * index.astype(jnp.float32)
    return jnp.cos(angle), jnp.sin(angle)


def densities(ur, ui, vr, vi):
    return vr * vr + vi * vi, ur * vr + ui * vi, ui * vr - ur * vi


def fields_of(n, kr, ki, scale):
    n = n * scale
    safe = jnp.where(n > 0.0, n, 1.0)
    power = jnp.where(n > 0.0, jnp.exp((2.0 / 3.0) * jnp.log(safe)), 0.0)
    return xi_factor * power - chemical, (-coupling * scale) * kr, (-coupling * scale) * ki


def local_part(field, ur, ui, vr, vi):
    potential, gap_real, gap_imag = field
    return (
        potential * ur + gap_real * vr - gap_imag * vi,
        potential * ui + gap_real * vi + gap_imag * vr,
        gap_real * ur + gap_imag * ui - potential * vr,
        gap_real * ui - gap_imag * ur - potential * vi,
    )


def copy_rows(x_ref, cloud, state, out_ref, first_row):
    planes, cells = x_ref.shape[3:]
    for k in range(4):
        rows = pl.ds(first_row + k * planes, planes)
        for t in range(cells // LANES):
            out_ref[rows, t, :] = x_ref[cloud, state, k, :, t * LANES : (t + 1) * LANES]


def take_kernel(mine, first, count, where_ref, x_ref, *refs):
    odd = lax.rem(where_ref[0], 2)
    out_ref = refs[-1]
    for s in range(count):
        copy_rows(x_ref, odd if mine else 1 - odd, first + s, out_ref, s * 4 * x_ref.shape[3])


def take(where, x, mine, first, count, *after):
    return pl.pallas_call(
        functools.partial(take_kernel, mine, first, count),
        out_shape=jax.ShapeDtypeStruct((count * 4 * x.shape[3], SUBS, LANES), x.dtype),
        in_specs=[SMEM, VMEM] + [ANYWHERE] * len(after),
        out_specs=VMEM,
        compiler_params=params(),
        name="take",
    )(where, x, *after)


def take_extra_kernel(where_ref, x_ref, *refs):
    out_ref, turned = refs[-2:]
    odd = lax.rem(where_ref[0], 2)
    per_group, _, planes, cells = x_ref.shape[1:]
    layers = REACH - 1

    def fill(cloud, lowest):
        for s in range(per_group):
            copy_rows(x_ref, cloud, s, turned, 0)
            for k in range(4):
                out_ref[(4 * s + k) * layers : (4 * s + k + 1) * layers] = turned[k * planes + lowest : k * planes + lowest + layers]

    @pl.when(odd == 1)
    def _():
        fill(0, planes - layers)

    @pl.when(odd == 0)
    def _():
        fill(1, 0)


def take_extra(where, x, *after):
    per_group, _, planes, _ = x.shape[1:]
    return pl.pallas_call(
        take_extra_kernel,
        out_shape=jax.ShapeDtypeStruct((per_group * 4 * (REACH - 1), SUBS, LANES), x.dtype),
        in_specs=[SMEM, VMEM] + [ANYWHERE] * len(after),
        out_specs=VMEM,
        scratch_shapes=[pltpu.VMEM((4 * planes, SUBS, LANES), x.dtype)],
        compiler_params=params(),
        name="take_extra",
    )(where, x, *after)


def join_kernel(count, *refs):
    out_ref = refs[-1]
    first = 0
    for ref in refs[:count]:
        out_ref[first : first + ref.shape[0]] = ref[...]
        first += ref.shape[0]


def join(pieces, *after):
    rows = sum(piece.shape[0] for piece in pieces)
    return pl.pallas_call(
        functools.partial(join_kernel, len(pieces)),
        out_shape=jax.ShapeDtypeStruct((rows, *pieces[0].shape[1:]), pieces[0].dtype),
        in_specs=[VMEM] * len(pieces) + [ANYWHERE] * len(after),
        out_specs=VMEM,
        compiler_params=params(),
        name="join",
    )(*pieces, *after)


def add_kernel(a_ref, b_ref, *refs):
    refs[-1][...] = a_ref[...] + b_ref[...]


def add(a, b, *after):
    return pl.pallas_call(
        add_kernel,
        out_shape=jax.ShapeDtypeStruct(a.shape, a.dtype),
        in_specs=[VMEM] * 2 + [ANYWHERE] * len(after),
        out_specs=VMEM,
        compiler_params=params(),
        name="add",
    )(a, b, *after)


def total_kernel(count, where_ref, *refs):
    odd = lax.rem(where_ref[0], 2)
    mine_ref, other_ref = refs[-2:]
    total = refs[0][...]
    for ref in refs[1:count]:
        total = total + ref[...]
    mine_ref[...] = jnp.where(odd == 1, total[1], total[0])
    other_ref[...] = jnp.where(odd == 1, total[0], total[1])


def total_of(where, terms, *after):
    return pl.pallas_call(
        functools.partial(total_kernel, len(terms)),
        out_shape=[jax.ShapeDtypeStruct(terms[0].shape[1:], terms[0].dtype)] * 2,
        in_specs=[SMEM] + [VMEM] * len(terms) + [ANYWHERE] * len(after),
        out_specs=[VMEM] * 2,
        compiler_params=params(),
        name="total",
    )(where, *terms, *after)


def raw_density_kernel(x_ref, *refs):
    out_ref = refs[-1]
    clouds, states, _, planes, cells = x_ref.shape
    for j in range(clouds):
        for t in range(cells // LANES):
            lanes = pl.ds(t * LANES, LANES)
            sums = [jnp.zeros((planes, LANES), jnp.float32)] * 3
            for s in range(states):
                terms = densities(*[x_ref[j, s, k, :, lanes] for k in range(4)])
                sums = [a + b for a, b in zip(sums, terms)]
            for f in range(3):
                out_ref[j, f, :, lanes] = sums[f]


def raw_density(x, *after):
    clouds, _, _, planes, cells = x.shape
    return pl.pallas_call(
        raw_density_kernel,
        out_shape=jax.ShapeDtypeStruct((clouds, 3, planes, cells), jnp.float32),
        in_specs=[VMEM] + [ANYWHERE] * len(after),
        out_specs=VMEM,
        compiler_params=params(),
        name="raw_density",
    )(x, *after)


def slots_of(cloud):
    return [jnp.where(cloud == 0, q, 3 - q) for q in range(4)]


def first_layer(cloud, slot, slab, planes, shift_ref):
    return jnp.where(cloud == 0, (slab - 3 + slot) * planes + shift_ref[0], (slab + slot) * planes - shift_ref[1])


def window_start(cloud, planes, reach, shift_ref):
    return jnp.where(cloud == 0, 3 * planes - reach - shift_ref[0], shift_ref[1] - reach)


def placed_fields_kernel(depth, scale, where_ref, shift_ref, wave_ref, *refs):
    mine_refs, other_refs = refs[0:4], refs[4:8]
    out_ref, held = refs[-2:]
    planes, cells = mine_refs[0].shape[1:]
    slab = where_ref[0]
    odd = lax.rem(slab, 2)
    count = out_ref.shape[1]
    totals = [jnp.zeros((count, SUBS, LANES), jnp.float32)] * 3
    for cloud, slot_refs in ((odd, mine_refs), (1 - odd, other_refs)):
        for slot, ref in zip(slots_of(cloud), slot_refs):
            cos, sin = phase(2 * wave_ref[cloud], first_layer(cloud, slot, slab, planes, shift_ref), depth)
            layers = pl.ds(slot * planes, planes)
            for t in range(cells // LANES):
                lanes = pl.ds(t * LANES, LANES)
                kr, ki = ref[1, :, lanes], ref[2, :, lanes]
                held[0, layers, t, :] = ref[0, :, lanes]
                held[1, layers, t, :] = kr * cos - ki * sin
                held[2, layers, t, :] = kr * sin + ki * cos
        start = window_start(cloud, planes, HALO, shift_ref)
        totals = [total + held[f, pl.ds(start, count)] for f, total in enumerate(totals)]
    for f, field in enumerate(fields_of(*totals, scale)):
        out_ref[f] = field


def placed_fields(where, shift, wave, mine, other, depth, scale, *after):
    planes = mine[0].shape[1]
    return pl.pallas_call(
        functools.partial(placed_fields_kernel, depth, scale),
        out_shape=jax.ShapeDtypeStruct((3, planes + 2 * HALO, SUBS, LANES), jnp.float32),
        in_specs=[SMEM] * 3 + [VMEM] * 8 + [ANYWHERE] * len(after),
        out_specs=VMEM,
        scratch_shapes=[pltpu.VMEM((3, 4 * planes, SUBS, LANES), jnp.float32)],
        compiler_params=params(),
        name="placed_fields",
    )(where, shift, wave, *mine, *other, *after)


def transverse(x, weights):
    rows = x.shape[0]
    flat = x.reshape(rows * SUBS, LANES)
    high = flat.astype(jnp.bfloat16)
    low = (flat - high.astype(jnp.float32)).astype(jnp.bfloat16)
    product = jnp.dot(jnp.concatenate([high, low], axis=1), weights, preferred_element_type=jnp.float32)
    sub = lax.broadcasted_iota(jnp.int32, (rows * SUBS, LANES), 0) % SUBS
    up = pltpu.roll(product[:, :LANES].reshape(rows, SUBS, LANES), 1, 1).reshape(rows * SUBS, LANES)
    down = pltpu.roll(product[:, 2 * LANES :].reshape(rows, SUBS, LANES), SUBS - 1, 1).reshape(rows * SUBS, LANES)
    result = product[:, LANES : 2 * LANES] + jnp.where(sub > 0, up, 0.0) + jnp.where(sub < SUBS - 1, down, 0.0)
    return result.reshape(rows, SUBS, LANES)


def kinetic(layers, weights):
    count = layers.shape[1] - 2 * HALO
    inner = layers[:, HALO : HALO + count]
    along = stencil[0] * inner
    for j in range(1, HALO + 1):
        along = along + stencil[j] * (layers[:, HALO - j : HALO - j + count] + layers[:, HALO + j : HALO + j + count])
    across = transverse(inner.reshape(-1, SUBS, LANES), weights).reshape(inner.shape)
    return -0.5 * along + (-0.5 / 180.0) * across


def turned(u_re, u_im, v_re, v_im, cos, sin):
    return u_re * cos - u_im * sin, u_re * sin + u_im * cos, v_re * cos + v_im * sin, v_im * cos - v_re * sin


def gather_kernel(depth, planes, mine, starts, where_ref, shift_ref, wave_ref, weights_ref, far_ref, second_ref, next_ref, own_ref, *refs):
    windows, boosted_ref, base_ref, turns = refs[-4:]
    slab = where_ref[0]
    odd = lax.rem(slab, 2)
    cloud = odd if mine else 1 - odd
    states, _, count = boosted_ref.shape[:3]
    layers = REACH - 1
    far_edge = jnp.where(cloud == 0, planes - layers, 0)
    own_edge = jnp.where(cloud == 0, 0, planes - layers)
    slots = slots_of(cloud)
    for slot in slots:
        for n, part in enumerate(phase(wave_ref[cloud], first_layer(cloud, slot, slab, planes, shift_ref), depth)):
            for z in range(planes):
                turns[n, slot * planes + z] = jnp.broadcast_to(part[z : z + 1], (SUBS, LANES))
    start = window_start(cloud, planes, HALO, shift_ref)

    for s in range(states):
        def fill(place, ref, row, pitch, number):
            for n in range(number):
                parts = [ref[row + k * pitch + n] for k in range(4)]
                for k, value in enumerate(turned(*parts, turns[0, place + n], turns[1, place + n])):
                    windows[s, k, place + n] = value

        rows = [(start_state + s) * 4 * planes for start_state in starts]
        if mine:
            fill(slots[0] * planes + far_edge, far_ref, (starts[0] + s) * 4 * layers, layers, layers)
        else:
            fill(slots[0] * planes + far_edge, far_ref, rows[0] + far_edge, planes, layers)
        fill(slots[1] * planes, second_ref, rows[1], planes, planes)
        fill(slots[2] * planes, next_ref, rows[2], planes, planes)
        fill(slots[3] * planes + own_edge, own_ref, rows[3] + own_edge, planes, layers)

        whole = windows[s, :, pl.ds(start, count + 2 * HALO)]
        values = whole[:, HALO : HALO + count]
        kin = kinetic(whole, weights_ref[...])
        boosted_ref[s] = values
        base_ref[s, 0] = values[0] + time_step * kin[1]
        base_ref[s, 1] = values[1] - time_step * kin[0]
        base_ref[s, 2] = values[2] - time_step * kin[3]
        base_ref[s, 3] = values[3] + time_step * kin[2]


def gather(where, shift, wave, weights, mine, pieces, count, planes, depth, *after):
    arrays, starts = zip(*pieces)
    shapes = [(count, 4, 4 * planes, SUBS, LANES)] + [(count, 4, planes, SUBS, LANES)] * 2
    return pl.pallas_call(
        functools.partial(gather_kernel, depth, planes, mine, starts),
        out_shape=[jax.ShapeDtypeStruct(shape, jnp.float32) for shape in shapes],
        in_specs=[SMEM] * 3 + [VMEM] * 5 + [ANYWHERE] * len(after),
        out_specs=[VMEM] * 3,
        scratch_shapes=[pltpu.VMEM((2, 4 * planes, SUBS, LANES), jnp.float32)],
        compiler_params=params(),
        name="gather",
    )(where, shift, wave, weights, *arrays, *after)


def density_kernel(pieces, fields, *refs):
    boosted_refs, base_refs = refs[:pieces], refs[pieces : 2 * pieces]
    out_ref, sums = refs[2 * pieces :]
    planes = sums.shape[1]
    for z in range(planes):
        field = [fields[f, HALO + z] for f in range(3)]
        total = [jnp.zeros((SUBS, LANES), jnp.float32)] * 3
        for boosted, base in zip(boosted_refs, base_refs):
            for s in range(boosted.shape[0]):
                part = local_part(field, *[boosted[s, k, z] for k in range(4)])
                pr = base[s, 0, z] + time_step * part[1]
                pi = base[s, 1, z] - time_step * part[0]
                hr = base[s, 2, z] + time_step * part[3]
                hi = base[s, 3, z] - time_step * part[2]
                total = [a + b for a, b in zip(total, densities(pr, pi, hr, hi))]
        for f in range(3):
            sums[f, z] = total[f]
    for f in range(3):
        for t in range(SUBS):
            out_ref[f, :, t * LANES : (t + 1) * LANES] = sums[f, :, t, :]


def density(fields, boosted, base, planes):
    pieces = len(boosted)
    return pl.pallas_call(
        functools.partial(density_kernel, pieces),
        out_shape=jax.ShapeDtypeStruct((3, planes, SUBS * LANES), jnp.float32),
        in_specs=[VMEM] * (1 + 2 * pieces),
        out_specs=VMEM,
        scratch_shapes=[pltpu.VMEM((3, planes, SUBS, LANES), jnp.float32)],
        compiler_params=params(),
        name="density",
    )(fields, *boosted, *base)


def free_kernel(places, where_ref, shift_ref, weights_ref, fields, *refs):
    pieces = len(places)
    windows, boosted_refs, base_refs = refs[:pieces], refs[pieces : 2 * pieces], refs[2 * pieces : 3 * pieces]
    free_ref, predicted_ref, window, combined = refs[3 * pieces :]
    planes = free_ref.shape[3]
    inner = pl.ds(HALO, planes)
    slab = where_ref[0]
    odd = lax.rem(slab, 2)
    edge = HALO + planes

    def predict(layer, field, boosted, base):
        part = local_part(field, *boosted)
        window[0, layer] = base[0] + time_step * part[1]
        window[1, layer] = base[1] - time_step * part[0]
        window[2, layer] = base[2] + time_step * part[3]
        window[3, layer] = base[3] - time_step * part[2]

    for (mine, first, count), boosted_window, boosted, base in zip(places, windows, boosted_refs, base_refs):
        j = odd if mine else 1 - odd
        start = window_start(j, planes, REACH, shift_ref)

        def one_state(s, _):
            sides = [boosted_window[s, :, pl.ds(start + first_side, 3 * HALO)] for first_side in (0, planes + HALO)]
            sides = jnp.concatenate(sides, axis=0)
            kin = kinetic(sides, weights_ref[...])
            for side, offset in ((0, 0), (1, edge)):
                for n in range(HALO):
                    value = [sides[4 * side + k, HALO + n] for k in range(4)]
                    turn = [kin[4 * side + k, n] for k in range(4)]
                    moved_on = [
                        value[0] + time_step * turn[1],
                        value[1] - time_step * turn[0],
                        value[2] - time_step * turn[3],
                        value[3] + time_step * turn[2],
                    ]
                    predict(offset + n, [fields[f, offset + n] for f in range(3)], value, moved_on)
            for z in range(planes):
                field = [fields[f, HALO + z] for f in range(3)]
                predict(HALO + z, field, [boosted[s, k, z] for k in range(4)], [base[s, k, z] for k in range(4)])
            kin = kinetic(window[...], weights_ref[...])
            mean = [0.5 * (boosted[s, k] + window[k, inner]) for k in range(4)]
            half = 0.5 * time_step
            combined[0] = mean[0] + half * kin[1]
            combined[1] = mean[1] - half * kin[0]
            combined[2] = mean[2] - half * kin[3]
            combined[3] = mean[3] + half * kin[2]
            for k in range(4):
                for t in range(SUBS):
                    lanes = pl.ds(t * LANES, LANES)
                    free_ref[0, first + s, k, :, lanes] = combined[k, :, t, :]
                    predicted_ref[0, first + s, k, :, lanes] = window[k, inner, t, :]
            return 0

        lax.fori_loop(0, count, one_state, 0)


def free_part(where, shift, weights, fields, windows, boosted, base, places, shape, planes):
    pieces = len(places)
    out = jax.ShapeDtypeStruct(shape, jnp.float32)
    return pl.pallas_call(
        functools.partial(free_kernel, tuple(places)),
        out_shape=[out] * 2,
        in_specs=[SMEM] * 2 + [VMEM] * (2 + 3 * pieces),
        out_specs=[VMEM] * 2,
        scratch_shapes=[
            pltpu.VMEM((4, planes + 2 * HALO, SUBS, LANES), jnp.float32),
            pltpu.VMEM((4, planes, SUBS, LANES), jnp.float32),
        ],
        compiler_params=params(),
        name="free_part",
    )(where, shift, weights, fields, *windows, *boosted, *base)


def last_kernel(scale, where_ref, *refs):
    partial_refs, pieces = refs[:-6], refs[-6:-2]
    out_ref, fields = refs[-2:]

    @pl.when(pl.program_id(0) == 0)
    def _():
        totals = []
        for f in range(3):
            total = partial_refs[0][f]
            for ref in partial_refs[1:]:
                total = total + ref[f]
            totals.append(total)
        for f, field in enumerate(fields_of(*totals, scale)):
            fields[f] = field

    half = 0.5 * time_step

    def write(free_ref, predicted_ref):
        for t in range(out_ref.shape[-1] // LANES):
            lanes = pl.ds(t * LANES, LANES)
            field = [fields[f, :, lanes] for f in range(3)]
            for s in range(out_ref.shape[1]):
                part = local_part(field, *[predicted_ref[0, s, k, :, lanes] for k in range(4)])
                out_ref[0, s, 0, :, lanes] = free_ref[0, s, 0, :, lanes] + half * part[1]
                out_ref[0, s, 1, :, lanes] = free_ref[0, s, 1, :, lanes] - half * part[0]
                out_ref[0, s, 2, :, lanes] = free_ref[0, s, 2, :, lanes] + half * part[3]
                out_ref[0, s, 3, :, lanes] = free_ref[0, s, 3, :, lanes] - half * part[2]

    mine = pl.program_id(0) == lax.rem(where_ref[0], 2)

    @pl.when(jnp.logical_not(mine))
    def _():
        write(pieces[0], pieces[2])

    @pl.when(mine)
    def _():
        write(pieces[1], pieces[3])


def last_part(where, partials, free, predicted, scale):
    shape = (2, *free[0].shape[1:])
    whole = lambda a: pl.BlockSpec(a.shape, lambda i: (0,) * a.ndim)
    return pl.pallas_call(
        functools.partial(last_kernel, scale),
        out_shape=jax.ShapeDtypeStruct(shape, jnp.float32),
        grid=(2,),
        in_specs=[SMEM] + [whole(a) for a in (*partials, *free, *predicted)],
        out_specs=pl.BlockSpec((1, *shape[1:]), lambda i: (i, 0, 0, 0, 0)),
        scratch_shapes=[pltpu.VMEM(partials[0].shape, jnp.float32)],
        compiler_params=params(),
        name="last_part",
    )(where, *partials, *free, *predicted)


def local(weights, cloud_states, cloud_shift, boost_wave):
    slab_count, group_count = lax.axis_size("slab"), lax.axis_size("grp")
    _, per_group, _, planes, cells = cloud_states.shape
    depth = planes * slab_count
    scale = 1.0 / (per_group * group_count)
    where = lax.axis_index("slab").astype(jnp.int32).reshape(1)

    even_on = lambda a: lax.ppermute(a, "slab", [(i, (i - 2 if i % 2 else i + 2) % slab_count) for i in range(slab_count)])
    odd_on = lambda a: lax.ppermute(a, "slab", [(i, (i + 2 if i % 2 else i - 2) % slab_count) for i in range(slab_count)])
    across = lambda a: lax.ppermute(a, "slab", [(i, (i + 3 if i % 2 else i - 3) % slab_count) for i in range(slab_count)])

    def paired(a, bit):
        return lax.ppermute(a, "grp", [(i, i ^ bit) for i in range(group_count)])

    def two_terms(a, *after):
        if group_count != 4:
            a = lax.psum(a, "grp")
            return [a, jnp.zeros_like(a)]
        a = add(a, paired(a, 1), *after)
        return [a, paired(a, 2)]

    def group_terms(a):
        if group_count > 4:
            return [lax.psum(a, "grp")]
        return [a] + [moved(a, "grp", d) for d in range(1, group_count)]

    chunks = [(0, per_group)]
    mine = [take(where, cloud_states, True, *chunk) for chunk in chunks]
    mine_second = [even_on(piece) for piece in mine]
    other = [take(where, cloud_states, False, *chunk) for chunk in chunks]
    other_second = [odd_on(piece) for piece in other]
    leaving = take_extra(where, cloud_states, mine[0])
    extra = across(leaving)
    terms = two_terms(raw_density(cloud_states, leaving))
    mine_sums, other_sums = total_of(where, terms, *mine_second, extra)

    mine_sums_second, other_sums_second, far_sums = even_on(mine_sums), odd_on(other_sums), across(other_sums)
    other_next = swapped(mine[0])
    other_far = swapped(join(mine_second, mine_sums))
    work = lambda *a: gather(where, cloud_shift, boost_wave, weights, *a, planes, depth)
    places, worked = [], []
    for n, (first, count) in enumerate(chunks):
        worked.append(work(False, [(other_far, first), (other_second[n], 0), (other_next, first), (other[n], 0)], count))
        places.append((False, first, count))
    joined = join([mine_sums_second, other_sums_second, mine_sums], far_sums, *[piece[1] for piece in worked])
    swapped_sums = swapped(joined)
    swapped_sums = [swapped_sums[3 * n : 3 * n + 3] for n in range(3)]
    mine_next = [swapped(join([piece], joined)) for piece in other_second]
    fields = placed_fields(
        where, cloud_shift, boost_wave, [far_sums, mine_sums_second, swapped_sums[1], mine_sums],
        [swapped_sums[0], other_sums_second, swapped_sums[2], other_sums], depth, scale,
    )
    for n, (first, count) in enumerate(chunks):
        worked.append(work(True, [(extra, first), (mine_second[n], 0), (mine_next[n], 0), (mine[n], 0)], count))
        places.append((True, first, count))
    windows, boosted, base = [list(part) for part in zip(*worked)]
    def free_of(n):
        return free_part(
            where, cloud_shift, weights, fields, windows[n : n + 1], boosted[n : n + 1], base[n : n + 1], places[n : n + 1],
            (1, *cloud_states.shape[1:]), planes,
        )

    first_parts = free_of(0)
    partials = two_terms(density(fields, boosted, base, planes), first_parts[0])
    free, predicted = zip(first_parts, free_of(1))
    return last_part(where, partials, free, predicted, scale)


def solution(mesh):
    states = P(None, "grp", None, "slab", None)
    weights = transverse_weights()
    step = jax.shard_map(local, mesh=mesh, in_specs=(P(), states, P(), P()), out_specs=states, check_vma=False)
    return lambda cloud_states, cloud_shift, boost_wave: step(weights, cloud_states, cloud_shift, boost_wave)
```

```python
import functools
import math

import jax
import jax.numpy as jnp
import numpy as np
from jax import lax
from jax.experimental import pallas as pl
from jax.experimental.pallas import tpu as pltpu
from jax.sharding import PartitionSpec as P

NY = 32
LANES = 128
SUBS = 8
HALO = 3
REACH = 2 * HALO
VMEM_BYTES = 40 * 1024 * 1024

stencil = (-49.0 / 18.0, 1.5, -0.15, 1.0 / 90.0)
coupling = 3.0
xi_factor = 1.2
chemical = 1.0
time_step = 0.1

VMEM = pl.BlockSpec(memory_space=pltpu.VMEM)
SMEM = pl.BlockSpec(memory_space=pltpu.SMEM)
ANYWHERE = pl.BlockSpec(memory_space=pl.ANY)


def params():
    return pltpu.CompilerParams(vmem_limit_bytes=VMEM_BYTES)


def moved(x, axis, by):
    peers = lax.axis_size(axis)
    return lax.ppermute(x, axis, [(i, (i + by) % peers) for i in range(peers)])


def swapped(x):
    peers = lax.axis_size("slab")
    return lax.ppermute(x, "slab", [(i, i ^ 1) for i in range(peers)])


def transverse_weights():
    whole = {0: -980.0, 1: 270.0, 2: -27.0, 3: 2.0}
    rows = LANES // NY
    weights = np.zeros((LANES, 3 * LANES), np.float32)
    for a in range(LANES):
        xa, ya = divmod(a, NY)
        for b in range(LANES):
            xb, yb = divmod(b, NY)
            for part, distance in ((0, xb + rows - xa), (1, xb - xa), (2, xb - rows - xa)):
                if ya == yb and abs(distance) <= HALO:
                    weights[a, part * LANES + b] += whole[abs(distance)]
            if xa == xb and 0 < abs(ya - yb) <= HALO:
                weights[a, LANES + b] += whole[abs(ya - yb)]
    return np.concatenate([weights, weights]).astype(jnp.bfloat16)


def phase(wave, first, depth):
    z = first + lax.broadcasted_iota(jnp.int32, (SUBS, LANES), 0)
    index = jnp.bitwise_and(wave * z, depth - 1)
    angle = (2.0 * math.pi / depth) * index.astype(jnp.float32)
    return jnp.cos(angle), jnp.sin(angle)


def densities(ur, ui, vr, vi):
    return vr * vr + vi * vi, ur * vr + ui * vi, ui * vr - ur * vi


def fields_of(n, kr, ki, scale):
    n = n * scale
    safe = jnp.where(n > 0.0, n, 1.0)
    power = jnp.where(n > 0.0, jnp.exp((2.0 / 3.0) * jnp.log(safe)), 0.0)
    return xi_factor * power - chemical, (-coupling * scale) * kr, (-coupling * scale) * ki


def local_part(field, ur, ui, vr, vi):
    potential, gap_real, gap_imag = field
    return (
        potential * ur + gap_real * vr - gap_imag * vi,
        potential * ui + gap_real * vi + gap_imag * vr,
        gap_real * ur + gap_imag * ui - potential * vr,
        gap_real * ui - gap_imag * ur - potential * vi,
    )


def copy_rows(x_ref, cloud, state, out_ref, first_row):
    planes, cells = x_ref.shape[3:]
    for k in range(4):
        rows = pl.ds(first_row + k * planes, planes)
        for t in range(cells // LANES):
            out_ref[rows, t, :] = x_ref[cloud, state, k, :, t * LANES : (t + 1) * LANES]


def take_kernel(mine, first, count, where_ref, x_ref, *refs):
    odd = lax.rem(where_ref[0], 2)
    out_ref = refs[-1]
    for s in range(count):
        copy_rows(x_ref, odd if mine else 1 - odd, first + s, out_ref, s * 4 * x_ref.shape[3])


def take(where, x, mine, first, count, *after):
    return pl.pallas_call(
        functools.partial(take_kernel, mine, first, count),
        out_shape=jax.ShapeDtypeStruct((count * 4 * x.shape[3], SUBS, LANES), x.dtype),
        in_specs=[SMEM, VMEM] + [ANYWHERE] * len(after),
        out_specs=VMEM,
        compiler_params=params(),
        name="take",
    )(where, x, *after)


def take_extra_kernel(where_ref, x_ref, *refs):
    out_ref, turned = refs[-2:]
    odd = lax.rem(where_ref[0], 2)
    per_group, _, planes, cells = x_ref.shape[1:]
    layers = REACH - 1

    def fill(cloud, lowest):
        for s in range(per_group):
            copy_rows(x_ref, cloud, s, turned, 0)
            for k in range(4):
                out_ref[(4 * s + k) * layers : (4 * s + k + 1) * layers] = turned[k * planes + lowest : k * planes + lowest + layers]

    @pl.when(odd == 1)
    def _():
        fill(0, planes - layers)

    @pl.when(odd == 0)
    def _():
        fill(1, 0)


def take_extra(where, x, *after):
    per_group, _, planes, _ = x.shape[1:]
    return pl.pallas_call(
        take_extra_kernel,
        out_shape=jax.ShapeDtypeStruct((per_group * 4 * (REACH - 1), SUBS, LANES), x.dtype),
        in_specs=[SMEM, VMEM] + [ANYWHERE] * len(after),
        out_specs=VMEM,
        scratch_shapes=[pltpu.VMEM((4 * planes, SUBS, LANES), x.dtype)],
        compiler_params=params(),
        name="take_extra",
    )(where, x, *after)


def join_kernel(count, *refs):
    out_ref = refs[-1]
    first = 0
    for ref in refs[:count]:
        out_ref[first : first + ref.shape[0]] = ref[...]
        first += ref.shape[0]


def join(pieces, *after):
    rows = sum(piece.shape[0] for piece in pieces)
    return pl.pallas_call(
        functools.partial(join_kernel, len(pieces)),
        out_shape=jax.ShapeDtypeStruct((rows, *pieces[0].shape[1:]), pieces[0].dtype),
        in_specs=[VMEM] * len(pieces) + [ANYWHERE] * len(after),
        out_specs=VMEM,
        compiler_params=params(),
        name="join",
    )(*pieces, *after)


def add_kernel(a_ref, b_ref, *refs):
    refs[-1][...] = a_ref[...] + b_ref[...]


def add(a, b, *after):
    return pl.pallas_call(
        add_kernel,
        out_shape=jax.ShapeDtypeStruct(a.shape, a.dtype),
        in_specs=[VMEM] * 2 + [ANYWHERE] * len(after),
        out_specs=VMEM,
        compiler_params=params(),
        name="add",
    )(a, b, *after)


def total_kernel(count, where_ref, *refs):
    odd = lax.rem(where_ref[0], 2)
    mine_ref, other_ref = refs[-2:]
    total = refs[0][...]
    for ref in refs[1:count]:
        total = total + ref[...]
    mine_ref[...] = jnp.where(odd == 1, total[1], total[0])
    other_ref[...] = jnp.where(odd == 1, total[0], total[1])


def total_of(where, terms, *after):
    return pl.pallas_call(
        functools.partial(total_kernel, len(terms)),
        out_shape=[jax.ShapeDtypeStruct(terms[0].shape[1:], terms[0].dtype)] * 2,
        in_specs=[SMEM] + [VMEM] * len(terms) + [ANYWHERE] * len(after),
        out_specs=[VMEM] * 2,
        compiler_params=params(),
        name="total",
    )(where, *terms, *after)


def raw_density_kernel(x_ref, *refs):
    out_ref = refs[-1]
    clouds, states, _, planes, cells = x_ref.shape
    for j in range(clouds):
        for t in range(cells // LANES):
            lanes = pl.ds(t * LANES, LANES)
            sums = [jnp.zeros((planes, LANES), jnp.float32)] * 3
            for s in range(states):
                terms = densities(*[x_ref[j, s, k, :, lanes] for k in range(4)])
                sums = [a + b for a, b in zip(sums, terms)]
            for f in range(3):
                out_ref[j, f, :, lanes] = sums[f]


def raw_density(x, *after):
    clouds, _, _, planes, cells = x.shape
    return pl.pallas_call(
        raw_density_kernel,
        out_shape=jax.ShapeDtypeStruct((clouds, 3, planes, cells), jnp.float32),
        in_specs=[VMEM] + [ANYWHERE] * len(after),
        out_specs=VMEM,
        compiler_params=params(),
        name="raw_density",
    )(x, *after)


def slots_of(cloud):
    return [jnp.where(cloud == 0, q, 3 - q) for q in range(4)]


def first_layer(cloud, slot, slab, planes, shift_ref):
    return jnp.where(cloud == 0, (slab - 3 + slot) * planes + shift_ref[0], (slab + slot) * planes - shift_ref[1])


def window_start(cloud, planes, reach, shift_ref):
    return jnp.where(cloud == 0, 3 * planes - reach - shift_ref[0], shift_ref[1] - reach)


def placed_fields_kernel(depth, scale, where_ref, shift_ref, wave_ref, *refs):
    mine_refs, other_refs = refs[0:4], refs[4:8]
    out_ref, held = refs[-2:]
    planes, cells = mine_refs[0].shape[1:]
    slab = where_ref[0]
    odd = lax.rem(slab, 2)
    count = out_ref.shape[1]
    totals = [jnp.zeros((count, SUBS, LANES), jnp.float32)] * 3
    for cloud, slot_refs in ((odd, mine_refs), (1 - odd, other_refs)):
        for slot, ref in zip(slots_of(cloud), slot_refs):
            cos, sin = phase(2 * wave_ref[cloud], first_layer(cloud, slot, slab, planes, shift_ref), depth)
            layers = pl.ds(slot * planes, planes)
            for t in range(cells // LANES):
                lanes = pl.ds(t * LANES, LANES)
                kr, ki = ref[1, :, lanes], ref[2, :, lanes]
                held[0, layers, t, :] = ref[0, :, lanes]
                held[1, layers, t, :] = kr * cos - ki * sin
                held[2, layers, t, :] = kr * sin + ki * cos
        start = window_start(cloud, planes, HALO, shift_ref)
        totals = [total + held[f, pl.ds(start, count)] for f, total in enumerate(totals)]
    for f, field in enumerate(fields_of(*totals, scale)):
        out_ref[f] = field


def placed_fields(where, shift, wave, mine, other, depth, scale, *after):
    planes = mine[0].shape[1]
    return pl.pallas_call(
        functools.partial(placed_fields_kernel, depth, scale),
        out_shape=jax.ShapeDtypeStruct((3, planes + 2 * HALO, SUBS, LANES), jnp.float32),
        in_specs=[SMEM] * 3 + [VMEM] * 8 + [ANYWHERE] * len(after),
        out_specs=VMEM,
        scratch_shapes=[pltpu.VMEM((3, 4 * planes, SUBS, LANES), jnp.float32)],
        compiler_params=params(),
        name="placed_fields",
    )(where, shift, wave, *mine, *other, *after)


def transverse(x, weights):
    rows = x.shape[0]
    flat = x.reshape(rows * SUBS, LANES)
    high = flat.astype(jnp.bfloat16)
    low = (flat - high.astype(jnp.float32)).astype(jnp.bfloat16)
    product = jnp.dot(jnp.concatenate([high, low], axis=1), weights, preferred_element_type=jnp.float32)
    sub = lax.broadcasted_iota(jnp.int32, (rows * SUBS, LANES), 0) % SUBS
    up = pltpu.roll(product[:, :LANES].reshape(rows, SUBS, LANES), 1, 1).reshape(rows * SUBS, LANES)
    down = pltpu.roll(product[:, 2 * LANES :].reshape(rows, SUBS, LANES), SUBS - 1, 1).reshape(rows * SUBS, LANES)
    result = product[:, LANES : 2 * LANES] + jnp.where(sub > 0, up, 0.0) + jnp.where(sub < SUBS - 1, down, 0.0)
    return result.reshape(rows, SUBS, LANES)


def kinetic(layers, weights):
    count = layers.shape[1] - 2 * HALO
    inner = layers[:, HALO : HALO + count]
    along = stencil[0] * inner
    for j in range(1, HALO + 1):
        along = along + stencil[j] * (layers[:, HALO - j : HALO - j + count] + layers[:, HALO + j : HALO + j + count])
    across = transverse(inner.reshape(-1, SUBS, LANES), weights).reshape(inner.shape)
    return -0.5 * along + (-0.5 / 180.0) * across


def turned(u_re, u_im, v_re, v_im, cos, sin):
    return u_re * cos - u_im * sin, u_re * sin + u_im * cos, v_re * cos + v_im * sin, v_im * cos - v_re * sin


def gather_kernel(depth, planes, mine, starts, where_ref, shift_ref, wave_ref, weights_ref, far_ref, second_ref, next_ref, own_ref, *refs):
    windows, boosted_ref, base_ref, turns = refs[-4:]
    slab = where_ref[0]
    odd = lax.rem(slab, 2)
    cloud = odd if mine else 1 - odd
    states, _, count = boosted_ref.shape[:3]
    layers = REACH - 1
    far_edge = jnp.where(cloud == 0, planes - layers, 0)
    own_edge = jnp.where(cloud == 0, 0, planes - layers)
    slots = slots_of(cloud)
    for slot in slots:
        for n, part in enumerate(phase(wave_ref[cloud], first_layer(cloud, slot, slab, planes, shift_ref), depth)):
            for z in range(planes):
                turns[n, slot * planes + z] = jnp.broadcast_to(part[z : z + 1], (SUBS, LANES))
    start = window_start(cloud, planes, HALO, shift_ref)

    for s in range(states):
        def fill(place, ref, row, pitch, number):
            for n in range(number):
                parts = [ref[row + k * pitch + n] for k in range(4)]
                for k, value in enumerate(turned(*parts, turns[0, place + n], turns[1, place + n])):
                    windows[s, k, place + n] = value

        rows = [(start_state + s) * 4 * planes for start_state in starts]
        if mine:
            fill(slots[0] * planes + far_edge, far_ref, (starts[0] + s) * 4 * layers, layers, layers)
        else:
            fill(slots[0] * planes + far_edge, far_ref, rows[0] + far_edge, planes, layers)
        fill(slots[1] * planes, second_ref, rows[1], planes, planes)
        fill(slots[2] * planes, next_ref, rows[2], planes, planes)
        fill(slots[3] * planes + own_edge, own_ref, rows[3] + own_edge, planes, layers)

        whole = windows[s, :, pl.ds(start, count + 2 * HALO)]
        values = whole[:, HALO : HALO + count]
        kin = kinetic(whole, weights_ref[...])
        boosted_ref[s] = values
        base_ref[s, 0] = values[0] + time_step * kin[1]
        base_ref[s, 1] = values[1] - time_step * kin[0]
        base_ref[s, 2] = values[2] - time_step * kin[3]
        base_ref[s, 3] = values[3] + time_step * kin[2]


def gather(where, shift, wave, weights, mine, pieces, count, planes, depth, *after):
    arrays, starts = zip(*pieces)
    shapes = [(count, 4, 4 * planes, SUBS, LANES)] + [(count, 4, planes, SUBS, LANES)] * 2
    return pl.pallas_call(
        functools.partial(gather_kernel, depth, planes, mine, starts),
        out_shape=[jax.ShapeDtypeStruct(shape, jnp.float32) for shape in shapes],
        in_specs=[SMEM] * 3 + [VMEM] * 5 + [ANYWHERE] * len(after),
        out_specs=[VMEM] * 3,
        scratch_shapes=[pltpu.VMEM((2, 4 * planes, SUBS, LANES), jnp.float32)],
        compiler_params=params(),
        name="gather",
    )(where, shift, wave, weights, *arrays, *after)


def density_kernel(pieces, fields, *refs):
    boosted_refs, base_refs = refs[:pieces], refs[pieces : 2 * pieces]
    out_ref, sums = refs[2 * pieces :]
    planes = sums.shape[1]
    for z in range(planes):
        field = [fields[f, HALO + z] for f in range(3)]
        total = [jnp.zeros((SUBS, LANES), jnp.float32)] * 3
        for boosted, base in zip(boosted_refs, base_refs):
            for s in range(boosted.shape[0]):
                part = local_part(field, *[boosted[s, k, z] for k in range(4)])
                pr = base[s, 0, z] + time_step * part[1]
                pi = base[s, 1, z] - time_step * part[0]
                hr = base[s, 2, z] + time_step * part[3]
                hi = base[s, 3, z] - time_step * part[2]
                total = [a + b for a, b in zip(total, densities(pr, pi, hr, hi))]
        for f in range(3):
            sums[f, z] = total[f]
    for f in range(3):
        for t in range(SUBS):
            out_ref[f, :, t * LANES : (t + 1) * LANES] = sums[f, :, t, :]


def density(fields, boosted, base, planes):
    pieces = len(boosted)
    return pl.pallas_call(
        functools.partial(density_kernel, pieces),
        out_shape=jax.ShapeDtypeStruct((3, planes, SUBS * LANES), jnp.float32),
        in_specs=[VMEM] * (1 + 2 * pieces),
        out_specs=VMEM,
        scratch_shapes=[pltpu.VMEM((3, planes, SUBS, LANES), jnp.float32)],
        compiler_params=params(),
        name="density",
    )(fields, *boosted, *base)


def free_kernel(places, where_ref, shift_ref, weights_ref, fields, *refs):
    pieces = len(places)
    windows, boosted_refs, base_refs = refs[:pieces], refs[pieces : 2 * pieces], refs[2 * pieces : 3 * pieces]
    free_ref, predicted_ref, window, combined = refs[3 * pieces :]
    planes = free_ref.shape[3]
    inner = pl.ds(HALO, planes)
    slab = where_ref[0]
    odd = lax.rem(slab, 2)
    edge = HALO + planes

    def predict(layer, field, boosted, base):
        part = local_part(field, *boosted)
        window[0, layer] = base[0] + time_step * part[1]
        window[1, layer] = base[1] - time_step * part[0]
        window[2, layer] = base[2] + time_step * part[3]
        window[3, layer] = base[3] - time_step * part[2]

    for (mine, first, count), boosted_window, boosted, base in zip(places, windows, boosted_refs, base_refs):
        j = odd if mine else 1 - odd
        start = window_start(j, planes, REACH, shift_ref)

        def one_state(s, _):
            sides = [boosted_window[s, :, pl.ds(start + first_side, 3 * HALO)] for first_side in (0, planes + HALO)]
            sides = jnp.concatenate(sides, axis=0)
            kin = kinetic(sides, weights_ref[...])
            for side, offset in ((0, 0), (1, edge)):
                for n in range(HALO):
                    value = [sides[4 * side + k, HALO + n] for k in range(4)]
                    turn = [kin[4 * side + k, n] for k in range(4)]
                    moved_on = [
                        value[0] + time_step * turn[1],
                        value[1] - time_step * turn[0],
                        value[2] - time_step * turn[3],
                        value[3] + time_step * turn[2],
                    ]
                    predict(offset + n, [fields[f, offset + n] for f in range(3)], value, moved_on)
            for z in range(planes):
                field = [fields[f, HALO + z] for f in range(3)]
                predict(HALO + z, field, [boosted[s, k, z] for k in range(4)], [base[s, k, z] for k in range(4)])
            kin = kinetic(window[...], weights_ref[...])
            mean = [0.5 * (boosted[s, k] + window[k, inner]) for k in range(4)]
            half = 0.5 * time_step
            combined[0] = mean[0] + half * kin[1]
            combined[1] = mean[1] - half * kin[0]
            combined[2] = mean[2] - half * kin[3]
            combined[3] = mean[3] + half * kin[2]
            for k in range(4):
                for t in range(SUBS):
                    lanes = pl.ds(t * LANES, LANES)
                    free_ref[0, first + s, k, :, lanes] = combined[k, :, t, :]
                    predicted_ref[0, first + s, k, :, lanes] = window[k, inner, t, :]
            return 0

        lax.fori_loop(0, count, one_state, 0)


def free_part(where, shift, weights, fields, windows, boosted, base, places, shape, planes):
    pieces = len(places)
    out = jax.ShapeDtypeStruct(shape, jnp.float32)
    return pl.pallas_call(
        functools.partial(free_kernel, tuple(places)),
        out_shape=[out] * 2,
        in_specs=[SMEM] * 2 + [VMEM] * (2 + 3 * pieces),
        out_specs=[VMEM] * 2,
        scratch_shapes=[
            pltpu.VMEM((4, planes + 2 * HALO, SUBS, LANES), jnp.float32),
            pltpu.VMEM((4, planes, SUBS, LANES), jnp.float32),
        ],
        compiler_params=params(),
        name="free_part",
    )(where, shift, weights, fields, *windows, *boosted, *base)


def last_kernel(scale, where_ref, *refs):
    partial_refs, pieces = refs[:-6], refs[-6:-2]
    out_ref, fields = refs[-2:]

    @pl.when(pl.program_id(0) == 0)
    def _():
        totals = []
        for f in range(3):
            total = partial_refs[0][f]
            for ref in partial_refs[1:]:
                total = total + ref[f]
            totals.append(total)
        for f, field in enumerate(fields_of(*totals, scale)):
            fields[f] = field

    half = 0.5 * time_step

    def write(free_ref, predicted_ref):
        for t in range(out_ref.shape[-1] // LANES):
            lanes = pl.ds(t * LANES, LANES)
            field = [fields[f, :, lanes] for f in range(3)]
            for s in range(out_ref.shape[1]):
                part = local_part(field, *[predicted_ref[0, s, k, :, lanes] for k in range(4)])
                out_ref[0, s, 0, :, lanes] = free_ref[0, s, 0, :, lanes] + half * part[1]
                out_ref[0, s, 1, :, lanes] = free_ref[0, s, 1, :, lanes] - half * part[0]
                out_ref[0, s, 2, :, lanes] = free_ref[0, s, 2, :, lanes] + half * part[3]
                out_ref[0, s, 3, :, lanes] = free_ref[0, s, 3, :, lanes] - half * part[2]

    mine = pl.program_id(0) == lax.rem(where_ref[0], 2)

    @pl.when(jnp.logical_not(mine))
    def _():
        write(pieces[0], pieces[2])

    @pl.when(mine)
    def _():
        write(pieces[1], pieces[3])


def last_part(where, partials, free, predicted, scale):
    shape = (2, *free[0].shape[1:])
    whole = lambda a: pl.BlockSpec(a.shape, lambda i: (0,) * a.ndim)
    return pl.pallas_call(
        functools.partial(last_kernel, scale),
        out_shape=jax.ShapeDtypeStruct(shape, jnp.float32),
        grid=(2,),
        in_specs=[SMEM] + [whole(a) for a in (*partials, *free, *predicted)],
        out_specs=pl.BlockSpec((1, *shape[1:]), lambda i: (i, 0, 0, 0, 0)),
        scratch_shapes=[pltpu.VMEM(partials[0].shape, jnp.float32)],
        compiler_params=params(),
        name="last_part",
    )(where, *partials, *free, *predicted)


def local(weights, cloud_states, cloud_shift, boost_wave):
    slab_count, group_count = lax.axis_size("slab"), lax.axis_size("grp")
    _, per_group, _, planes, cells = cloud_states.shape
    depth = planes * slab_count
    scale = 1.0 / (per_group * group_count)
    where = lax.axis_index("slab").astype(jnp.int32).reshape(1)

    even_on = lambda a: lax.ppermute(a, "slab", [(i, (i - 2 if i % 2 else i + 2) % slab_count) for i in range(slab_count)])
    odd_on = lambda a: lax.ppermute(a, "slab", [(i, (i + 2 if i % 2 else i - 2) % slab_count) for i in range(slab_count)])
    across = lambda a: lax.ppermute(a, "slab", [(i, (i + 3 if i % 2 else i - 3) % slab_count) for i in range(slab_count)])

    def paired(a, bit):
        return lax.ppermute(a, "grp", [(i, i ^ bit) for i in range(group_count)])

    def two_terms(a, *after):
        if group_count != 4:
            a = lax.psum(a, "grp")
            return [a, jnp.zeros_like(a)]
        a = add(a, paired(a, 1), *after)
        return [a, paired(a, 2)]

    def group_terms(a):
        if group_count > 4:
            return [lax.psum(a, "grp")]
        return [a] + [moved(a, "grp", d) for d in range(1, group_count)]

    chunks = [(0, per_group)]
    mine = [take(where, cloud_states, True, *chunk) for chunk in chunks]
    mine_second = [even_on(piece) for piece in mine]
    other = [take(where, cloud_states, False, *chunk) for chunk in chunks]
    other_second = [odd_on(piece) for piece in other]
    terms = two_terms(raw_density(cloud_states, *mine, *other))
    extra = across(take_extra(where, cloud_states, mine[0]))
    mine_sums, other_sums = total_of(where, terms, extra)

    mine_sums_second, other_sums_second, far_sums = even_on(mine_sums), odd_on(other_sums), across(other_sums)
    other_next = swapped(mine[0])
    other_far = swapped(join(mine_second, mine_sums))
    work = lambda *a: gather(where, cloud_shift, boost_wave, weights, *a, planes, depth)
    places, worked = [], []
    for n, (first, count) in enumerate(chunks):
        worked.append(work(False, [(other_far, first), (other_second[n], 0), (other_next, first), (other[n], 0)], count))
        places.append((False, first, count))
    joined = join([mine_sums_second, other_sums_second, mine_sums], far_sums, *[piece[1] for piece in worked])
    swapped_sums = swapped(joined)
    swapped_sums = [swapped_sums[3 * n : 3 * n + 3] for n in range(3)]
    mine_next = [swapped(join([piece], joined)) for piece in other_second]
    fields = placed_fields(
        where, cloud_shift, boost_wave, [far_sums, mine_sums_second, swapped_sums[1], mine_sums],
        [swapped_sums[0], other_sums_second, swapped_sums[2], other_sums], depth, scale,
    )
    for n, (first, count) in enumerate(chunks):
        worked.append(work(True, [(extra, first), (mine_second[n], 0), (mine_next[n], 0), (mine[n], 0)], count))
        places.append((True, first, count))
    windows, boosted, base = [list(part) for part in zip(*worked)]
    def free_of(n):
        return free_part(
            where, cloud_shift, weights, fields, windows[n : n + 1], boosted[n : n + 1], base[n : n + 1], places[n : n + 1],
            (1, *cloud_states.shape[1:]), planes,
        )

    first_parts = free_of(0)
    partials = two_terms(density(fields, boosted, base, planes), first_parts[0])
    free, predicted = zip(first_parts, free_of(1))
    return last_part(where, partials, free, predicted, scale)


def solution(mesh):
    states = P(None, "grp", None, "slab", None)
    weights = transverse_weights()
    step = jax.shard_map(local, mesh=mesh, in_specs=(P(), states, P(), P()), out_specs=states, check_vma=False)
    return lambda cloud_states, cloud_shift, boost_wave: step(weights, cloud_states, cloud_shift, boost_wave)
```
